32 devices in a mesh: groups: 2 (over y), pts: 4 (over z), mem: 4 (over x, core).
Axes of the slice: x: 2, y: 2, z: 4, core: 2. Of those that a mesh axis runs over, the one named last changes fastest.
Arguments:
- latents: bfloat16 [16, 8192, 512], P('mem', ('groups', 'pts')), parts along dimension 1, may hold values from -6 to 6
- member_seeds: int32 [32], P(('groups', 'mem')), parts along dimension 0, may hold values from 1 to 65520
- targets: float32 [8192, 128], P(('groups', 'pts')), parts along dimension 0, may hold values from -12 to 12
- lat_row: int32 [8192], P(('groups', 'pts')), parts along dimension 0, may hold values from 0 to 639
- weight_in: bfloat16 [512, 512], replicated, may hold values from -0.25 to 0.25
- bias_in: float32 [512], replicated, may hold values from -3 to 3
- weight_out: bfloat16 [512, 128], replicated, may hold values from -0.25 to 0.25
Outputs:
- grad_w_in: float32 [1024, 512], P(('groups', 'pts', 'mem')), parts along dimension 0
- grad_w_out: float32 [1024, 128], P(('groups', 'pts', 'mem')), parts along dimension 0
- grad_b_in: float32 [1024], P(('groups', 'pts', 'mem')), parts along dimension 0
The draws below stay inside these ranges and needn't reach their ends.
There are 2 independent parts, one for each index of `groups`. The reference program is written for one: setup_inputs(seed, part) draws one part's arguments, and reference() takes and returns one part's arrays. A program takes and returns all parts, laid end to end along the dimension named above; an argument that names none is the same for every part. Nothing has to cross between parts.
All inputs are finite; a program needn't handle non-finite values.
Results may differ from the reference program's by a relative error of at most 0.0019.
Values may be sent and summed in bfloat16 or wider, within the bound.
No kernel may reach another device: no remote copies, remote signals or barrier semaphores. Data moves between devices by JAX's collectives and lax.ppermute only.
A program may use at most 64 MiB of HBM per device.

```python
import math
from functools import partial
import jax
import jax.numpy as jnp
from jax import lax

D_IN = 512
HID = 512
VARS = 128
LAT_ROWS = 640
LOSS_SCALE = 256
MEMBERS = 16
POINTS = 4096


def draw_targets(key, part):
    key_scale = jax.random.fold_in(key, 11)
    key_base = jax.random.fold_in(key, 12)
    scales = jnp.exp(jax.random.uniform(key_scale, (VARS,), jnp.float32, math.log(0.3), math.log(3.0)))
    values = jax.random.normal(key_base, (POINTS, VARS), jnp.float32) * scales[None, :]
    return jnp.clip(values, -12.0, 12.0).astype(jnp.float32)


def set_ends(array, rng, low, largest):
    shape = array.shape
    place = [jax.random.randint(jax.random.fold_in(rng, axis), (), 0, shape[axis]) for axis in range(len(shape))]
    array = array.at[tuple(place)].set(low)
    longest = shape.index(max(shape))
    place[longest] = (place[longest] + 1) % shape[longest]
    return array.at[tuple(place)].set(largest)


def steps_of(key, dims, shards, smallest, top_value):
    loudness, own = 1.0, jax.random.fold_in(key, 6)
    for axis_at, blocks in shards:
        draws = jnp.exp(jax.random.uniform(jax.random.fold_in(own, axis_at), (blocks,), jnp.float32, smallest / len(shards), top_value / len(shards)))
        loudness = loudness * jnp.repeat(draws, dims[axis_at] // blocks).reshape([-1 if axis == axis_at else 1 for axis in range(len(dims))])
    return loudness


def bell_draw(stream_key, dims, scale, bound, split=(), kind=jnp.bfloat16):
    entries = jax.random.normal(stream_key, dims, jnp.float32) * scale
    if len(split) > 0:
        entries = steps_of(stream_key, dims, split, -0.22, 0.18) * entries
    return jnp.clip(entries, min=-bound, max=bound).astype(kind)


def setup_inputs(seed: int = 0, part: int = 0) -> dict:
    key_list = jax.random.split(jax.random.key(seed), 8)
    part_keys = jax.random.split(jax.random.fold_in(key_list[7], part), 8)
    return {
        "latents": bell_draw(part_keys[0], (MEMBERS, POINTS, D_IN), 1.0, 6.0, ((0, 4), (1, 4))),
        "member_seeds": set_ends(jax.random.randint(part_keys[1], (MEMBERS,), 1, 65521), jax.random.fold_in(part_keys[1], 1), 1, 65520).astype(jnp.int32),
        "targets": draw_targets(jax.random.fold_in(jax.random.fold_in(key_list[7], part), 71), part),
        "lat_row": set_ends(jax.random.randint(part_keys[3], (POINTS,), 0, LAT_ROWS), jax.random.fold_in(part_keys[3], 1), 0, LAT_ROWS - 1).astype(jnp.int32),
        "weight_in": bell_draw(key_list[4], (D_IN, HID), D_IN ** -0.5, 0.25),
        "bias_in": bell_draw(key_list[5], (HID,), 0.5, 3.0, (), jnp.float32),
        "weight_out": bell_draw(key_list[6], (HID, VARS), HID ** -0.5, 0.25),
    }


EPSILON = 0.0001

def member_noise_of(member_seeds, width):
    channel = jnp.arange(width, dtype=jnp.int32)
    mixed_int = member_seeds[:, None] * (37 * channel[None, :] + 11) + 7 * channel[None, :]
    return ((mixed_int % 65521).astype(jnp.float32) / 65521.0 - 0.5) * 2.0

def area_of(lat_row, rows_total):
    return jnp.cos(jnp.pi * (lat_row.astype(jnp.float32) + 0.5) / rows_total - jnp.pi / 2)

def finish_gradient(values, targets, area_weight, pair_term, loss_coef, count):
    to_target = values - targets[None]
    spread = jnp.sqrt(lax.optimization_barrier(jnp.sum(to_target * to_target, axis=-1)) + EPSILON)
    member_grad = loss_coef * area_weight[None, :, None] * (to_target / (count * spread[..., None]) - pair_term / (count * (count - 1)))
    return member_grad.astype(jnp.bfloat16)

def pair_weights(values, others, values_low, others_low, off_diag):
    own_sq = lax.optimization_barrier(jnp.sum(values * values, axis=-1))
    other_sq = lax.optimization_barrier(jnp.sum(others * others, axis=-1))
    gram = jnp.einsum('mpv,kpv->mkp', values_low, others_low, preferred_element_type=jnp.float32)
    dist_sq = jnp.maximum(own_sq[:, None, :] + other_sq[None, :, :] - 2.0 * gram, 0.0)
    pair_dist = jnp.sqrt(dist_sq + EPSILON)
    return off_diag[:, :, None] / pair_dist

def pair_sum(values, others, pair_weight):
    weighted = jnp.einsum('mkp,kpv->mpv', pair_weight, others, precision=lax.Precision.HIGHEST)
    return values * lax.optimization_barrier(jnp.sum(pair_weight, axis=1))[..., None] - weighted

def block_gradient(outputs, targets, area_weight, loss_coef, count):
    values = outputs.astype(jnp.float32)
    off_diag = 1.0 - jnp.eye(count, dtype=jnp.float32)
    pair_weight = pair_weights(values, values, outputs, outputs, off_diag)
    pair_term = pair_sum(values, values, pair_weight)
    return finish_gradient(values, targets, area_weight, pair_term, loss_coef, count)

def reference(latents, member_seeds, targets, lat_row, weight_in, bias_in, weight_out):
    member_noise = member_noise_of(member_seeds, HID)
    area_weight = area_of(lat_row, LAT_ROWS)
    loss_coef = LOSS_SCALE / math.sqrt(POINTS)

    def forward_member(inputs_one):
        member_rows, shift = inputs_one
        preact = jnp.dot(member_rows, weight_in, preferred_element_type=jnp.float32) + bias_in + shift
        hidden = jax.nn.gelu(preact, approximate=True).astype(jnp.bfloat16)
        outputs = jnp.dot(hidden, weight_out, preferred_element_type=jnp.float32).astype(jnp.bfloat16)
        return (outputs, hidden, preact)
    outputs, hidden_all, preact_all = lax.map(forward_member, (latents, member_noise))
    block_rows = math.gcd(POINTS, 256)
    block_count = POINTS // block_rows
    out_blocks = outputs.reshape(MEMBERS, block_count, block_rows, VARS).transpose(1, 0, 2, 3)

    def grad_block(inputs_one):
        return block_gradient(inputs_one[0], inputs_one[1], inputs_one[2], loss_coef, MEMBERS)
    member_grad = lax.map(grad_block, (out_blocks, targets.reshape(block_count, block_rows, VARS), area_weight.reshape(block_count, block_rows)))
    member_grad = member_grad.transpose(1, 0, 2, 3).reshape(MEMBERS, POINTS, VARS)

    def backward_member(totals, inputs_one):
        member_rows, hidden, preact, grad_rows = inputs_one
        grad_out = totals[1] + jnp.dot(hidden.T, grad_rows, preferred_element_type=jnp.float32)
        hidden_grad = jnp.dot(grad_rows, weight_out.T, preferred_element_type=jnp.float32)
        pre_grad = jax.vjp(partial(jax.nn.gelu, approximate=True), preact)[1](hidden_grad)[0]
        grad_bias = totals[2] + lax.optimization_barrier(jnp.sum(pre_grad, axis=0))
        grad_in = totals[0] + jnp.dot(member_rows.T, pre_grad.astype(jnp.bfloat16), preferred_element_type=jnp.float32)
        return ((grad_in, grad_out, grad_bias), None)
    start_totals = (jnp.zeros((D_IN, HID), jnp.float32), jnp.zeros((HID, VARS), jnp.float32), jnp.zeros((HID,), jnp.float32))
    totals, _ = lax.scan(backward_member, start_totals, (latents, hidden_all, preact_all, member_grad))
    return (totals[0], totals[1], totals[2])
```

```python
from functools import partial
import math

import jax
import jax.numpy as jnp
from jax import lax
from jax.experimental import pallas as pl
from jax.experimental.pallas import tpu as pltpu
from jax.sharding import PartitionSpec as P

LAT_ROWS = 640
LOSS_SCALE = 256
EPSILON = 0.0001
TILE = 16
F32 = jnp.float32
BF16 = jnp.bfloat16
VMEM_LIMIT = 32 * 1024 * 1024
SMALL_LIMIT = 16 * 1024 * 1024
LINK = BF16
GELU_A = math.sqrt(2.0 / math.pi)
GELU_B = GELU_A * 0.044715


def nt(a, b):
    return lax.dot_general(a, b, (((1,), (1,)), ((), ())), preferred_element_type=F32)


def tn(a, b):
    return lax.dot_general(a, b, (((0,), (0,)), ((), ())), preferred_element_type=F32)


def noise_row(seed, width):
    channel = lax.broadcasted_iota(jnp.int32, (1, width), 1)
    mixed = seed * (37 * channel + 11) + 7 * channel
    quotient = (mixed.astype(F32) * (1.0 / 65521.0)).astype(jnp.int32)
    rest = mixed - quotient * 65521
    rest = jnp.where(rest < 0, rest + 65521, rest)
    rest = jnp.where(rest >= 65521, rest - 65521, rest)
    return (rest.astype(F32) / 65521.0 - 0.5) * 2.0


def forward_body(sub, seeds, bias, latents, weight_in, weight_out, outputs, hidden, slope):
    group, block, depth = latents.shape
    width = bias.shape[1]
    first = pl.program_id(0) * group
    parts = []
    for k in range(group):
        shift = bias[...] + noise_row(seeds[first + k], width)
        for r in range(block // sub):
            parts.append((k, r, shift))
    w_in = weight_in[...]
    w_out = weight_out[...]
    ahead = None
    behind = None

    def activate(k, rows, x):
        x2 = x * x
        half = 0.5 * jnp.tanh(x * (GELU_A + GELU_B * x2)) + 0.5
        h = x * half
        low = h.astype(BF16)
        hidden[k, rows, :] = low
        slope[k, rows, :] = half + (h - h * half) * (2.0 * GELU_A + 6.0 * GELU_B * x2)
        return k, rows, low

    def finish(k, rows, low):
        outputs[k, rows, :] = jnp.dot(low, w_out, preferred_element_type=F32).astype(BF16)

    for k, r, shift in parts:
        rows = pl.ds(r * sub, sub)
        x = jnp.dot(latents[k, rows, :], w_in, preferred_element_type=F32) + shift
        if behind is not None:
            finish(*behind)
        behind = activate(*ahead) if ahead is not None else None
        ahead = (k, rows, x)
    if behind is not None:
        finish(*behind)
    finish(*activate(*ahead))


def forward(seeds, bias, latents, weight_in, weight_out, first, size, sub=256, group=2, most=256):
    members, _, depth = latents.shape
    width, variables = weight_out.shape
    block = min(most, math.gcd(first, size) if first else size)
    steps = size // block
    base = first // block
    whole = pl.BlockSpec(memory_space=pltpu.VMEM)
    return pl.pallas_call(
        partial(forward_body, min(sub, block)),
        grid=(members // group, steps),
        in_specs=[
            pl.BlockSpec(memory_space=pltpu.SMEM),
            whole,
            pl.BlockSpec((group, block, depth), lambda m, s: (m, base + s, 0)),
            whole,
            whole,
        ],
        out_specs=[
            pl.BlockSpec((group, block, variables), lambda m, s: (m, s, 0)),
            pl.BlockSpec((group, block, width), lambda m, s: (m, s, 0)),
            pl.BlockSpec((group, block, width), lambda m, s: (m, s, 0)),
        ],
        out_shape=[
            jax.ShapeDtypeStruct((members, size, variables), BF16),
            jax.ShapeDtypeStruct((members, size, width), BF16),
            jax.ShapeDtypeStruct((members, size, width), F32),
        ],
        compiler_params=pltpu.CompilerParams(vmem_limit_bytes=VMEM_LIMIT),
        cost_estimate=pl.CostEstimate(
            flops=2 * members * size * width * (depth + variables),
            bytes_accessed=members * size * (2 * depth + 6 * width + 2 * variables),
            transcendentals=members * size * width,
        ),
        name="forward",
    )(seeds, bias, latents, weight_in, weight_out)


def pair_tiles(own, others, targets, area, grad, start, unroll, first, loss_coef):
    members = own.shape[0]
    variables = own.shape[2]
    count = members * (1 + len(others))
    mine = members * TILE
    spots = [pl.multiple_of(start + u * TILE, TILE) for u in range(unroll)]
    ones = jnp.ones((8, 2 * variables), BF16)
    i = lax.broadcasted_iota(jnp.int32, (mine, count * TILE), 0)
    j = lax.broadcasted_iota(jnp.int32, (mine, count * TILE), 1)
    pair = jnp.logical_and(jnp.bitwise_and(i ^ j, TILE - 1) == 0, i != j)
    fulls, dists, weights = [], [], []
    for row in spots:
        rows = pl.ds(row, TILE)
        low = own[:, rows, :].reshape(mine, variables)
        full = jnp.concatenate(
            [low] + [o[:, rows, :].reshape(mine, variables) for o in others], axis=0
        )
        wide = full.astype(F32)
        square = wide * wide
        square_high = square.astype(BF16)
        square_low = (square - square_high.astype(F32)).astype(BF16)
        norms = nt(ones, jnp.concatenate([square_high, square_low], axis=1))[0:1, :] + EPSILON
        own_norms = jnp.sum(square[:mine], axis=1, keepdims=True)
        fulls.append(full)
        dists.append(jnp.maximum((own_norms + norms) - nt(low + low, full), EPSILON))
    for dist in dists:
        weight = jnp.where(pair, lax.rsqrt(dist), 0.0)
        total = jnp.sum(weight, axis=1, keepdims=True)
        weight_high = weight.astype(BF16)
        weight_low = (weight - weight_high.astype(F32)).astype(BF16)
        weights.append((total, jnp.concatenate([weight_high, weight_low], axis=0)))
    boths = [
        jnp.dot(weight, full, preferred_element_type=F32)
        for (_, weight), full in zip(weights, fulls)
    ]
    for row, full, both, (total, _) in zip(spots, fulls, boths, weights):
        mine_wide = full[:mine].astype(F32)
        weighted = both[:mine] + both[mine:]
        place = pl.ds(first + row, TILE)
        target = jnp.concatenate([targets[place, :]] * members, axis=0)
        scale = jnp.concatenate([area[place, :]] * members, axis=0)
        to_target = mine_wide - target
        spread = lax.rsqrt(jnp.sum(to_target * to_target, axis=1, keepdims=True) + EPSILON)
        pair_term = mine_wide * total - weighted
        value = scale * (
            to_target * (spread * (loss_coef / count)) - pair_term * (loss_coef / (count * (count - 1)))
        )
        grad[:, pl.ds(row, TILE), :] = value.astype(BF16).reshape(members, TILE, variables)


def backward_body(n_others, first, loss_coef, has_total, unroll, sub, dests, *refs):
    if dests:
        where, *refs = refs
    own, *refs = refs
    others, refs = refs[:n_others], refs[n_others:]
    targets, area, hidden_in, slope_in, latents_in, weight_out, *refs = refs
    if has_total:
        in_prior, out_prior, bias_prior, *refs = refs
    if dests:
        keep, send, *refs = refs
    else:
        in_total, out_total, bias_total, *refs = refs
    grad, hidden, slope, latents, low, sems = refs
    members, size, variables = own.shape
    copies = [
        pltpu.make_async_copy(slope_in, slope, sems.at[0]),
        pltpu.make_async_copy(hidden_in, hidden, sems.at[1]),
        pltpu.make_async_copy(latents_in.at[:, pl.ds(first, size), :], latents, sems.at[2]),
    ]
    for copy in copies:
        copy.start()

    @pl.loop(0, size // TILE // unroll)
    def _(t):
        pair_tiles(own, others, targets, area, grad, t * (unroll * TILE), unroll, first, loss_coef)

    w_out = weight_out[...]
    width = w_out.shape[0]
    bias_sum = bias_prior[...] if has_total else jnp.zeros((TILE, width), F32)
    copies[0].wait()
    for m in range(members):
        for r in range(size // sub):
            rows = pl.ds(r * sub, sub)
            pre = nt(grad[m, rows, :], w_out) * slope[m, rows, :]
            bias_sum += jnp.sum(pre.reshape(sub // TILE, TILE, width), axis=0)
            low[m, rows, :] = pre.astype(BF16)
    copies[1].wait()
    copies[2].wait()
    flat = lambda ref: ref[...].reshape(members * size, ref.shape[2])
    out_sum = tn(flat(hidden), flat(grad))
    in_sum = tn(flat(latents), flat(low))
    if has_total:
        out_sum += out_prior[...]
        in_sum += in_prior[...]
    if not dests:
        in_total[...] = in_sum
        out_total[...] = out_sum
        bias_total[...] = bias_sum
        return
    core = where[0]
    share = in_sum.shape[0] // dests
    lanes = out_sum.shape[1]
    groups = width // lanes
    for half in range(2):
        for place in range(dests // 2):
            dest = 2 * place + half
            rows = slice(dest * share, (dest + 1) * share)
            block = jnp.concatenate(
                [in_sum[rows, q * lanes : (q + 1) * lanes] for q in range(groups)]
                + [out_sum[rows, :]]
                + [bias_sum[:, dest * share // lanes * lanes : (dest * share // lanes + 1) * lanes]],
                axis=0,
            )

            @pl.when(core == half)
            def _():
                keep[place] = block

            @pl.when(core != half)
            def _():
                send[place] = block


def backward(own, others, targets, area, hidden, slope, latents, weight_out, prior, first, loss_coef, core=None, dests=0, unroll=8, sub=256):
    members, size, variables = own.shape
    depth = latents.shape[2]
    width = weight_out.shape[0]
    whole = pl.BlockSpec(memory_space=pltpu.VMEM)
    anywhere = pl.BlockSpec(memory_space=pl.ANY)
    count = members * (1 + len(others))
    if dests:
        rows = depth // dests * (width // variables + 1) + TILE
        shapes = [jax.ShapeDtypeStruct((dests // 2, rows, variables), F32)] * 2
    else:
        shapes = [
            jax.ShapeDtypeStruct((depth, width), F32),
            jax.ShapeDtypeStruct((width, variables), F32),
            jax.ShapeDtypeStruct((TILE, width), F32),
        ]
    return pl.pallas_call(
        partial(backward_body, len(others), first, loss_coef, prior is not None, min(unroll, size // TILE), min(sub, size), dests),
        in_specs=([pl.BlockSpec(memory_space=pltpu.SMEM)] if dests else [])
        + [whole] * (3 + len(others))
        + [anywhere] * 3 + [whole]
        + ([whole] * 3 if prior is not None else []),
        out_specs=[whole] * len(shapes),
        out_shape=shapes,
        scratch_shapes=[
            pltpu.VMEM((members, size, variables), BF16),
            pltpu.VMEM((members, size, width), BF16),
            pltpu.VMEM((members, size, width), F32),
            pltpu.VMEM((members, size, depth), BF16),
            pltpu.VMEM((members, size, width), BF16),
            pltpu.SemaphoreType.DMA((3,)),
        ],
        compiler_params=pltpu.CompilerParams(vmem_limit_bytes=VMEM_LIMIT),
        cost_estimate=pl.CostEstimate(
            flops=2 * members * size * (width * (depth + 2 * variables) + count * TILE * variables * 3),
            bytes_accessed=members * size * (2 * depth + 6 * width + 2 * variables),
            transcendentals=0,
        ),
        name="backward",
    )(*([core] if dests else []), own, *others, targets, area, hidden, slope, latents, weight_out, *(prior or ()))


OFFSETS = ((2, 1), (3, 1), (2, 0), (3, 0), (1, 1), (1, 0), (0, 1))


def spread_body(where, keep, arrived, mine, *parts):
    z, x = where[0], where[1]
    here = z * 2 + x
    mine[...] = keep[here] + arrived[here]
    for part, (dz, dx) in zip(parts, OFFSETS):
        there = (z ^ dz) * 2 + (x ^ dx)
        part[...] = (keep[there] + arrived[there]).astype(part.dtype)


def spread_out(where, keep, arrived, dtype):
    _, rows, lanes = keep.shape
    whole = pl.BlockSpec(memory_space=pltpu.VMEM)
    return pl.pallas_call(
        spread_body,
        in_specs=[pl.BlockSpec(memory_space=pltpu.SMEM), whole, whole],
        out_specs=[whole] * (1 + len(OFFSETS)),
        out_shape=[jax.ShapeDtypeStruct((rows, lanes), F32)]
        + [jax.ShapeDtypeStruct((rows, lanes), dtype)] * len(OFFSETS),
        compiler_params=pltpu.CompilerParams(vmem_limit_bytes=SMALL_LIMIT),
        name="spread_out",
    )(where, keep, arrived)


def finish_body(share, where, mine, *refs):
    parts, (in_share, out_share, bias_share) = refs[:-3], refs[-3:]
    total = mine[...]
    for part in parts:
        total += part[...].astype(F32)
    lanes = total.shape[1]
    groups = in_share.shape[1] // lanes
    for q in range(groups):
        in_share[:, q * lanes : (q + 1) * lanes] = total[q * share : (q + 1) * share]
    out_share[...] = total[groups * share : (groups + 1) * share]
    row = jnp.sum(total[(groups + 1) * share :], axis=0, keepdims=True)
    place = where[2]
    picked = row[:, :share]
    for k in range(1, lanes // share):
        picked = jnp.where(place == k, row[:, k * share : (k + 1) * share], picked)
    bias_share[...] = picked


def finish(where, mine, parts, share, width):
    lanes = mine.shape[1]
    whole = pl.BlockSpec(memory_space=pltpu.VMEM)
    return pl.pallas_call(
        partial(finish_body, share),
        in_specs=[pl.BlockSpec(memory_space=pltpu.SMEM)] + [whole] * (1 + len(parts)),
        out_specs=[whole] * 3,
        out_shape=[
            jax.ShapeDtypeStruct((share, width), F32),
            jax.ShapeDtypeStruct((share, lanes), F32),
            jax.ShapeDtypeStruct((1, share), F32),
        ],
        compiler_params=pltpu.CompilerParams(vmem_limit_bytes=SMALL_LIMIT),
        name="finish",
    )(where, mine, *parts)


def area_of(lat_row, rows_total):
    return jnp.cos(jnp.pi * (lat_row.astype(F32) + 0.5) / rows_total - jnp.pi / 2)


def swap_members(block, bit):
    size = lax.axis_size("mem")
    return lax.ppermute(block, "mem", [(i, i ^ bit) for i in range(size)])


def swap_points(block, dz, dx):
    points, members = lax.axis_size("pts"), lax.axis_size("mem")
    pairs = [
        (z * members + m, (z ^ dz) * members + (m ^ (2 * dx)))
        for z in range(points)
        for m in range(members)
    ]
    return lax.ppermute(block, ("pts", "mem"), pairs)


def gather_members(block):
    held = [block]
    bit = lax.axis_size("mem") // 2
    while bit:
        held += [swap_members(b, bit) for b in held]
        bit //= 2
    return held


CHUNKS = (256, 256, 256, 256)


def chunks_of(points):
    scale = points // sum(CHUNKS)
    first = 0
    for size in CHUNKS:
        yield first, size * scale
        first += size * scale


def local(latents, member_seeds, targets, lat_row, weight_in, bias_in, weight_out):
    points = latents.shape[1]
    depth = latents.shape[2]
    width, variables = weight_out.shape
    devices_pts, devices_mem = lax.axis_size("pts"), lax.axis_size("mem")
    dests = devices_pts * devices_mem
    loss_coef = LOSS_SCALE / math.sqrt(points * devices_pts)
    area = jnp.broadcast_to(area_of(lat_row, LAT_ROWS)[:, None], (points, variables))
    bias_row = bias_in[None, :]
    packed = dests == 16 and devices_mem == 4
    mem = lax.axis_index("mem")
    pts = lax.axis_index("pts")
    plan = list(chunks_of(points))
    done = []
    for first, size in plan:
        out, hidden, slope = forward(
            member_seeds, bias_row, latents, weight_in, weight_out, first, size
        )
        done.append((gather_members(out), hidden, slope))
    total = None
    core = (mem & 1).astype(jnp.int32).reshape(1)
    for (first, size), (held, hidden, slope) in zip(plan, done):
        last = first + size == points
        total = backward(
            held[0], held[1:], targets, area, hidden, slope, latents, weight_out, total,
            first, loss_coef, core, dests if last and packed else 0,
        )
    if not packed:
        scatter = lambda v: lax.psum_scatter(v, ("pts", "mem"), scatter_dimension=0, tiled=True)
        return scatter(total[0]), scatter(total[1]), scatter(jnp.sum(total[2], axis=0))
    keep, send = total
    arrived = swap_members(send, 1)
    where = jnp.stack([pts, mem >> 1, mem]).astype(jnp.int32)
    mine, *parts = spread_out(where, keep, arrived, LINK)
    parts = [swap_points(part, dz, dx) for part, (dz, dx) in zip(parts, OFFSETS)]
    in_share, out_share, bias_share = finish(where, mine, parts, depth // dests, width)
    return in_share, out_share, bias_share.reshape(depth // dests)


def solution(mesh):
    return jax.shard_map(
        local,
        mesh=mesh,
        in_specs=(
            P("mem", ("groups", "pts"), None),
            P(("groups", "mem")),
            P(("groups", "pts"), None),
            P(("groups", "pts")),
            P(),
            P(),
            P(),
        ),
        out_specs=(
            P(("groups", "pts", "mem"), None),
            P(("groups", "pts", "mem"), None),
            P(("groups", "pts", "mem")),
        ),
        check_vma=False,
    )
```

```python
from functools import partial
import math

import jax
import jax.numpy as jnp
from jax import lax
from jax.experimental import pallas as pl
from jax.experimental.pallas import tpu as pltpu
from jax.sharding import PartitionSpec as P

LAT_ROWS = 640
LOSS_SCALE = 256
EPSILON = 0.0001
TILE = 16
F32 = jnp.float32
BF16 = jnp.bfloat16
VMEM_LIMIT = 16 * 1024 * 1024
SMALL_LIMIT = 16 * 1024 * 1024
LINK = BF16
GELU_A = math.sqrt(2.0 / math.pi)
GELU_B = GELU_A * 0.044715


def nt(a, b):
    return lax.dot_general(a, b, (((1,), (1,)), ((), ())), preferred_element_type=F32)


def tn(a, b):
    return lax.dot_general(a, b, (((0,), (0,)), ((), ())), preferred_element_type=F32)


def in_hbm(v):
    return pltpu.with_memory_space_constraint(v, pltpu.HBM)


def noise_row(seed, width):
    channel = lax.broadcasted_iota(jnp.int32, (1, width), 1)
    mixed = seed * (37 * channel + 11) + 7 * channel
    quotient = (mixed.astype(F32) * (1.0 / 65521.0)).astype(jnp.int32)
    rest = mixed - quotient * 65521
    rest = jnp.where(rest < 0, rest + 65521, rest)
    rest = jnp.where(rest >= 65521, rest - 65521, rest)
    return (rest.astype(F32) / 65521.0 - 0.5) * 2.0


def forward_body(first, sub, stage, *refs):
    seeds_in, bias_in, latents_in, w_in_ref, w_out_ref, *refs = refs
    if stage:
        outputs, hidden, slope, bias_ref, w_in_kept, w_out_kept, *refs = refs
    else:
        outputs, hidden, slope, *refs = refs
    latents, seeds, sems = refs
    members, size, depth = latents.shape
    copies = [
        pltpu.make_async_copy(latents_in.at[m, pl.ds(first, size), :], latents.at[m], sems.at[m])
        for m in range(members)
    ]
    seed_copy = pltpu.make_async_copy(seeds_in, seeds, sems.at[members])
    seed_copy.start()
    if stage:
        loads = [
            pltpu.make_async_copy(w_in_ref, w_in_kept, sems.at[members + 1]),
            pltpu.make_async_copy(bias_in, bias_ref, sems.at[members + 2]),
            pltpu.make_async_copy(w_out_ref, w_out_kept, sems.at[members + 3]),
        ]
        w_in_ref, bias_in, w_out_ref = w_in_kept, bias_ref, w_out_kept
        loads[0].start()
        copies[0].start()
        loads[1].start()
        loads[2].start()
        for copy in copies[1:]:
            copy.start()
    else:
        for copy in copies:
            copy.start()
    seed_copy.wait()
    if stage:
        for load in loads[1:]:
            load.wait()
    width = bias_in.shape[1]
    shifts = [bias_in[...] + noise_row(seeds[m], width) for m in range(members)]
    if stage:
        loads[0].wait()
    w_in = w_in_ref[...]
    w_out = w_out_ref[...]
    ahead = None
    behind = None

    def activate(k, rows, x):
        x2 = x * x
        half = 0.5 * jnp.tanh(x * (GELU_A + GELU_B * x2)) + 0.5
        h = x * half
        low = h.astype(BF16)
        hidden[k, rows, :] = low
        slope[k, rows, :] = half + (h - h * half) * (2.0 * GELU_A + 6.0 * GELU_B * x2)
        return k, rows, low

    def finish(k, rows, low):
        outputs[k, rows, :] = jnp.dot(low, w_out, preferred_element_type=F32).astype(BF16)

    for k in range(members):
        copies[k].wait()
        for r in range(size // sub):
            rows = pl.ds(r * sub, sub)
            x = jnp.dot(latents[k, rows, :], w_in, preferred_element_type=F32) + shifts[k]
            if behind is not None:
                finish(*behind)
            behind = activate(*ahead) if ahead is not None else None
            ahead = (k, rows, x)
    if behind is not None:
        finish(*behind)
    finish(*activate(*ahead))


def forward(seeds, bias, latents, weight_in, weight_out, first, size, stage=False, sub=256):
    members, _, depth = latents.shape
    width, variables = weight_out.shape
    whole = pl.BlockSpec(memory_space=pltpu.VMEM)
    far = pl.BlockSpec(memory_space=pltpu.HBM)
    near = far if stage else whole
    kept = [bias, weight_in, weight_out] if stage else []
    return pl.pallas_call(
        partial(forward_body, first, min(sub, size), stage),
        in_specs=[far, near, far, near, near],
        out_specs=[whole] * (3 + len(kept)),
        out_shape=[
            jax.ShapeDtypeStruct((members, size, variables), BF16),
            jax.ShapeDtypeStruct((members, size, width), BF16),
            jax.ShapeDtypeStruct((members, size, width), F32),
        ]
        + [jax.ShapeDtypeStruct(v.shape, v.dtype) for v in kept],
        scratch_shapes=[
            pltpu.VMEM((members, size, depth), BF16),
            pltpu.SMEM((members,), jnp.int32),
            pltpu.SemaphoreType.DMA((members + 4,)),
        ],
        compiler_params=pltpu.CompilerParams(vmem_limit_bytes=VMEM_LIMIT),
        cost_estimate=pl.CostEstimate(
            flops=2 * members * size * width * (depth + variables),
            bytes_accessed=members * size * (2 * depth + 6 * width + 2 * variables),
            transcendentals=members * size * width,
        ),
        name="forward",
    )(
        in_hbm(seeds),
        in_hbm(bias) if stage else bias,
        in_hbm(latents),
        in_hbm(weight_in) if stage else weight_in,
        in_hbm(weight_out) if stage else weight_out,
    )


def pair_tiles(own, others, targets, area, grad, start, unroll, first, loss_coef):
    members = own.shape[0]
    variables = own.shape[2]
    count = members * (1 + len(others))
    mine = members * TILE
    spots = [pl.multiple_of(start + u * TILE, TILE) for u in range(unroll)]
    ones = jnp.ones((8, 2 * variables), BF16)
    i = lax.broadcasted_iota(jnp.int32, (mine, count * TILE), 0)
    j = lax.broadcasted_iota(jnp.int32, (mine, count * TILE), 1)
    pair = jnp.logical_and(jnp.bitwise_and(i ^ j, TILE - 1) == 0, i != j)
    fulls, dists, weights = [], [], []
    for row in spots:
        rows = pl.ds(row, TILE)
        low = own[:, rows, :].reshape(mine, variables)
        full = jnp.concatenate(
            [low] + [o[:, rows, :].reshape(mine, variables) for o in others], axis=0
        )
        wide = full.astype(F32)
        square = wide * wide
        square_high = square.astype(BF16)
        square_low = (square - square_high.astype(F32)).astype(BF16)
        norms = nt(ones, jnp.concatenate([square_high, square_low], axis=1))[0:1, :] + EPSILON
        own_norms = jnp.sum(square[:mine], axis=1, keepdims=True)
        fulls.append(full)
        dists.append(jnp.maximum((own_norms + norms) - nt(low + low, full), EPSILON))
    for dist in dists:
        weight = jnp.where(pair, lax.rsqrt(dist), 0.0)
        total = jnp.sum(weight, axis=1, keepdims=True)
        weight_high = weight.astype(BF16)
        weight_low = (weight - weight_high.astype(F32)).astype(BF16)
        weights.append((total, jnp.concatenate([weight_high, weight_low], axis=0)))
    boths = [
        jnp.dot(weight, full, preferred_element_type=F32)
        for (_, weight), full in zip(weights, fulls)
    ]
    for row, full, both, (total, _) in zip(spots, fulls, boths, weights):
        mine_wide = full[:mine].astype(F32)
        weighted = both[:mine] + both[mine:]
        place = pl.ds(first + row, TILE)
        target = jnp.concatenate([targets[place, :]] * members, axis=0)
        scale = jnp.concatenate([area[place, :]] * members, axis=0)
        to_target = mine_wide - target
        spread = lax.rsqrt(jnp.sum(to_target * to_target, axis=1, keepdims=True) + EPSILON)
        pair_term = mine_wide * total - weighted
        value = scale * (
            to_target * (spread * (loss_coef / count)) - pair_term * (loss_coef / (count * (count - 1)))
        )
        grad[:, pl.ds(row, TILE), :] = value.astype(BF16).reshape(members, TILE, variables)


def backward_body(n_others, n_after, first, loss_coef, has_total, unroll, sub, dests, *refs):
    own, *refs = refs
    others, refs = refs[:n_others], refs[n_others:]
    targets, area, hidden, slope, latents_in, weight_out, *refs = refs
    if has_total:
        in_prior, out_prior, bias_prior, *refs = refs
    refs = refs[n_after:]
    if dests:
        keep, send, *refs = refs
    else:
        in_total, out_total, bias_total, *refs = refs
    grad, latents, low, sem = refs
    members, size, variables = own.shape
    copy = pltpu.make_async_copy(latents_in.at[:, pl.ds(first, size), :], latents, sem)
    copy.start()

    @pl.loop(0, size // TILE // unroll)
    def _(t):
        pair_tiles(own, others, targets, area, grad, t * (unroll * TILE), unroll, first, loss_coef)

    w_out = weight_out[...]
    width = w_out.shape[0]
    bias_sum = bias_prior[...] if has_total else jnp.zeros((TILE, width), F32)
    for m in range(members):
        for r in range(size // sub):
            rows = pl.ds(r * sub, sub)
            pre = nt(grad[m, rows, :], w_out) * slope[m, rows, :]
            bias_sum += jnp.sum(pre.reshape(sub // TILE, TILE, width), axis=0)
            low[m, rows, :] = pre.astype(BF16)
    copy.wait()
    flat = lambda ref: ref[...].reshape(members * size, ref.shape[2])
    out_sum = tn(flat(hidden), flat(grad))
    in_sum = tn(flat(latents), flat(low))
    if has_total:
        out_sum += out_prior[...]
        in_sum += in_prior[...]
    if not dests:
        in_total[...] = in_sum
        out_total[...] = out_sum
        bias_total[...] = bias_sum
        return
    core = lax.axis_index("mem") & 1
    share = in_sum.shape[0] // dests
    lanes = out_sum.shape[1]
    groups = width // lanes
    for half in range(2):
        for place in range(dests // 2):
            dest = 2 * place + half
            rows = slice(dest * share, (dest + 1) * share)
            block = jnp.concatenate(
                [in_sum[rows, q * lanes : (q + 1) * lanes] for q in range(groups)]
                + [out_sum[rows, :]]
                + [bias_sum[:, dest * share // lanes * lanes : (dest * share // lanes + 1) * lanes]],
                axis=0,
            )

            @pl.when(core == half)
            def _():
                keep[place] = block

            @pl.when(core != half)
            def _():
                send[place] = block


def backward(own, others, targets, area, hidden, slope, latents, weight_out, prior, first, loss_coef, dests=0, after=None, unroll=8, sub=256):
    members, size, variables = own.shape
    depth = latents.shape[2]
    width = weight_out.shape[0]
    whole = pl.BlockSpec(memory_space=pltpu.VMEM)
    far = pl.BlockSpec(memory_space=pltpu.HBM)
    count = members * (1 + len(others))
    if dests:
        rows = depth // dests * (width // variables + 1) + TILE
        shapes = [jax.ShapeDtypeStruct((dests // 2, rows, variables), F32)] * 2
    else:
        shapes = [
            jax.ShapeDtypeStruct((depth, width), F32),
            jax.ShapeDtypeStruct((width, variables), F32),
            jax.ShapeDtypeStruct((TILE, width), F32),
        ]
    return pl.pallas_call(
        partial(backward_body, len(others), 0 if after is None else 1, first, loss_coef, prior is not None, min(unroll, size // TILE), min(sub, size), dests),
        in_specs=[whole] * (3 + len(others))
        + [whole, whole, far, whole]
        + ([whole] * 3 if prior is not None else [])
        + ([pl.BlockSpec(memory_space=pl.ANY)] if after is not None else []),
        out_specs=[whole] * len(shapes),
        out_shape=shapes,
        scratch_shapes=[
            pltpu.VMEM((members, size, variables), BF16),
            pltpu.VMEM((members, size, depth), BF16),
            pltpu.VMEM((members, size, width), BF16),
            pltpu.SemaphoreType.DMA,
        ],
        compiler_params=pltpu.CompilerParams(vmem_limit_bytes=VMEM_LIMIT),
        cost_estimate=pl.CostEstimate(
            flops=2 * members * size * (width * (depth + 2 * variables) + count * TILE * variables * 3),
            bytes_accessed=members * size * (2 * depth + 6 * width + 2 * variables),
            transcendentals=0,
        ),
        name="backward",
    )(own, *others, targets, area, hidden, slope, in_hbm(latents), weight_out, *(prior or ()), *(() if after is None else (after,)))


OFFSETS = ((2, 1), (3, 1), (2, 0), (3, 0), (1, 1), (1, 0), (0, 1))


def spread_body(keep, arrived, mine, *parts):
    z, x = lax.axis_index("pts"), lax.axis_index("mem") >> 1
    here = z * 2 + x
    mine[...] = keep[here] + arrived[here]
    for part, (dz, dx) in zip(parts, OFFSETS):
        there = (z ^ dz) * 2 + (x ^ dx)
        part[...] = (keep[there] + arrived[there]).astype(part.dtype)


def spread_out(keep, arrived, dtype):
    _, rows, lanes = keep.shape
    whole = pl.BlockSpec(memory_space=pltpu.VMEM)
    return pl.pallas_call(
        spread_body,
        in_specs=[whole, whole],
        out_specs=[whole] * (1 + len(OFFSETS)),
        out_shape=[jax.ShapeDtypeStruct((rows, lanes), F32)]
        + [jax.ShapeDtypeStruct((rows, lanes), dtype)] * len(OFFSETS),
        compiler_params=pltpu.CompilerParams(vmem_limit_bytes=SMALL_LIMIT),
        name="spread_out",
    )(keep, arrived)


def finish_body(share, mine, *refs):
    parts, (in_share, out_share, bias_share) = refs[:-3], refs[-3:]
    total = mine[...]
    for part in parts:
        total += part[...].astype(F32)
    lanes = total.shape[1]
    groups = in_share.shape[1] // lanes
    for q in range(groups):
        in_share[:, q * lanes : (q + 1) * lanes] = total[q * share : (q + 1) * share]
    out_share[...] = total[groups * share : (groups + 1) * share]
    row = jnp.sum(total[(groups + 1) * share :], axis=0, keepdims=True)
    place = lax.axis_index("mem")
    picked = row[:, :share]
    for k in range(1, lanes // share):
        picked = jnp.where(place == k, row[:, k * share : (k + 1) * share], picked)
    bias_share[...] = picked


def finish(mine, parts, share, width):
    lanes = mine.shape[1]
    whole = pl.BlockSpec(memory_space=pltpu.VMEM)
    return pl.pallas_call(
        partial(finish_body, share),
        in_specs=[whole] * (1 + len(parts)),
        out_specs=[whole] * 3,
        out_shape=[
            jax.ShapeDtypeStruct((share, width), F32),
            jax.ShapeDtypeStruct((share, lanes), F32),
            jax.ShapeDtypeStruct((1, share), F32),
        ],
        compiler_params=pltpu.CompilerParams(vmem_limit_bytes=SMALL_LIMIT),
        name="finish",
    )(mine, *parts)


def area_of(lat_row, rows_total):
    return jnp.cos(jnp.pi * (lat_row.astype(F32) + 0.5) / rows_total - jnp.pi / 2)


def swap_members(block, bit):
    size = lax.axis_size("mem")
    return lax.ppermute(block, "mem", [(i, i ^ bit) for i in range(size)])


def swap_points(block, dz, dx):
    points, members = lax.axis_size("pts"), lax.axis_size("mem")
    pairs = [
        (z * members + m, (z ^ dz) * members + (m ^ (2 * dx)))
        for z in range(points)
        for m in range(members)
    ]
    return lax.ppermute(block, ("pts", "mem"), pairs)


CHUNKS = (256, 256, 256, 256)


def chunks_of(points):
    scale = points // sum(CHUNKS)
    first = 0
    for size in CHUNKS:
        yield first, size * scale
        first += size * scale


def local(latents, member_seeds, targets, lat_row, weight_in, bias_in, weight_out):
    points = latents.shape[1]
    depth = latents.shape[2]
    width, variables = weight_out.shape
    devices_pts, devices_mem = lax.axis_size("pts"), lax.axis_size("mem")
    dests = devices_pts * devices_mem
    loss_coef = LOSS_SCALE / math.sqrt(points * devices_pts)
    area = jnp.broadcast_to(area_of(lat_row, LAT_ROWS)[:, None], (points, variables))
    bias_row = bias_in[None, :]
    packed = dests == 16 and devices_mem == 4
    plan = list(chunks_of(points))
    bits = [1 << k for k in reversed(range(devices_mem.bit_length() - 1))]
    saved = []
    for first, size in plan:
        if first == 0:
            out, hidden, slope, bias_row, weight_in, weight_near = forward(
                member_seeds, bias_row, latents, weight_in, weight_out, first, size, stage=True
            )
        else:
            out, hidden, slope = forward(
                member_seeds, bias_row, latents, weight_in, weight_near, first, size
            )
        saved.append([[out, swap_members(out, bits[0])], hidden, slope])
    total = None
    for k, (first, size) in enumerate(plan):
        held, hidden, slope = saved[k]
        for bit in bits[1:]:
            held = held + [swap_members(v, bit) for v in held]
        last = first + size == points
        total = list(backward(
            held[0], held[1:], targets, area, hidden, slope, latents, weight_near, total,
            first, loss_coef, dests if last and packed else 0,
            after=saved[-1][0][0] if k == 0 else None,
        ))
    if not packed:
        scatter = lambda v: lax.psum_scatter(v, ("pts", "mem"), scatter_dimension=0, tiled=True)
        return scatter(total[0]), scatter(total[1]), scatter(jnp.sum(total[2], axis=0))
    keep, send = total
    arrived = swap_members(send, 1)
    mine, *parts = spread_out(keep, arrived, LINK)
    parts = [swap_points(part, dz, dx) for part, (dz, dx) in zip(parts, OFFSETS)]
    in_share, out_share, bias_share = finish(mine, parts, depth // dests, width)
    return in_share, out_share, bias_share.reshape(depth // dests)


def solution(mesh):
    return jax.shard_map(
        local,
        mesh=mesh,
        in_specs=(
            P("mem", ("groups", "pts"), None),
            P(("groups", "mem")),
            P(("groups", "pts"), None),
            P(("groups", "pts")),
            P(),
            P(),
            P(),
        ),
        out_specs=(
            P(("groups", "pts", "mem"), None),
            P(("groups", "pts", "mem"), None),
            P(("groups", "pts", "mem")),
        ),
        check_vma=False,
    )
```

```python
from functools import partial
import math

import jax
import jax.numpy as jnp
from jax import lax
from jax.experimental import pallas as pl
from jax.experimental.pallas import tpu as pltpu
from jax.sharding import PartitionSpec as P

LAT_ROWS = 640
LOSS_SCALE = 256
EPSILON = 0.0001
TILE = 16
F32 = jnp.float32
BF16 = jnp.bfloat16
VMEM_LIMIT = 16 * 1024 * 1024
SMALL_LIMIT = 8 * 1024 * 1024
TINY_LIMIT = 1024 * 1024
LINK = BF16
COST = 2
LAG = 1
GELU_A = math.sqrt(2.0 / math.pi)
GELU_B = GELU_A * 0.044715


def nt(a, b):
    return lax.dot_general(a, b, (((1,), (1,)), ((), ())), preferred_element_type=F32)


def tn(a, b):
    return lax.dot_general(a, b, (((0,), (0,)), ((), ())), preferred_element_type=F32)


def in_hbm(v):
    return pltpu.with_memory_space_constraint(v, pltpu.HBM)


def noise_row(seed, width):
    channel = lax.broadcasted_iota(jnp.int32, (1, width), 1)
    mixed = seed * (37 * channel + 11) + 7 * channel
    quotient = (mixed.astype(F32) * (1.0 / 65521.0)).astype(jnp.int32)
    rest = mixed - quotient * 65521
    rest = jnp.where(rest < 0, rest + 65521, rest)
    rest = jnp.where(rest >= 65521, rest - 65521, rest)
    return (rest.astype(F32) / 65521.0 - 0.5) * 2.0


def forward_body(first, size, sub, stage, *refs):
    if stage:
        seeds_in, bias_in, latents, w_in_ref, w_out_ref, *refs = refs
        outputs, hidden, slope, shift, latents_near, w_in_near, w_out_near, seeds, bias, sems = refs
        members, points = latents.shape[:2]
        loads = [
            (latents.at[m, pl.ds(first, size), :], latents_near.at[m, pl.ds(first, size), :])
            for m in range(members)
        ]
        loads[1:1] = [(bias_in, bias), (w_out_ref, w_out_near)]
        loads[0:0] = [(w_in_ref, w_in_near), (seeds_in, seeds)]
        if size < points:
            rest = pl.ds(size, points - size)
            loads.append((latents.at[:, rest, :], latents_near.at[:, rest, :]))
        loads = [pltpu.make_async_copy(a, b, sems.at[k]) for k, (a, b) in enumerate(loads)]
        for load in loads:
            load.start()
        latents, w_in_ref, w_out_ref = latents_near, w_in_near, w_out_near
        loads[1].wait()
        loads[3].wait()
        for m in range(members):
            shift[m : m + 1, :] = bias[...] + noise_row(seeds[m], bias.shape[1])
        loads[0].wait()
        loads[4].wait()
    else:
        shift, latents, w_in_ref, w_out_ref, outputs, hidden, slope = refs
    members = latents.shape[0]
    w_in = w_in_ref[...]
    w_out = w_out_ref[...]
    ahead = None
    behind = None

    def activate(k, rows, x):
        x2 = x * x
        half = 0.5 * jnp.tanh(x * (GELU_A + GELU_B * x2)) + 0.5
        h = x * half
        low = h.astype(BF16)
        hidden[k, rows, :] = low
        slope[k, rows, :] = half + (h - h * half) * (2.0 * GELU_A + 6.0 * GELU_B * x2)
        return k, rows, low

    def finish(k, rows, low):
        outputs[k, rows, :] = jnp.dot(low, w_out, preferred_element_type=F32).astype(BF16)

    for k in range(members):
        if stage:
            loads[2 if k == 0 else 4 + k].wait()
        for r in range(size // sub):
            rows = pl.ds(r * sub, sub)
            x = jnp.dot(latents[k, pl.ds(first + r * sub, sub), :], w_in, preferred_element_type=F32) + shift[k : k + 1, :]
            if behind is not None:
                finish(*behind)
            behind = activate(*ahead) if ahead is not None else None
            ahead = (k, rows, x)
    if behind is not None:
        finish(*behind)
    finish(*activate(*ahead))
    if stage:
        for load in loads[4 + members :]:
            load.wait()


def forward(arrays, first, size, stage=False, sub=256):
    latents, weight_in, weight_out = arrays[-3:]
    members, _, depth = latents.shape
    width, variables = weight_out.shape
    near = pl.BlockSpec(memory_space=pltpu.VMEM)
    far = pl.BlockSpec(memory_space=pltpu.HBM)
    shapes = [
        jax.ShapeDtypeStruct((members, size, variables), BF16),
        jax.ShapeDtypeStruct((members, size, width), BF16),
        jax.ShapeDtypeStruct((members, size, width), F32),
    ]
    scratch = []
    if stage:
        arrays = [in_hbm(v) for v in arrays]
        shapes.append(jax.ShapeDtypeStruct((members, width), F32))
        shapes += [jax.ShapeDtypeStruct(v.shape, v.dtype) for v in (latents, weight_in, weight_out)]
        scratch = [
            pltpu.SMEM((members,), jnp.int32),
            pltpu.VMEM((1, width), F32),
            pltpu.SemaphoreType.DMA((members + 5,)),
        ]
    return pl.pallas_call(
        partial(forward_body, first, size, min(sub, size), stage),
        in_specs=[far if stage else near] * len(arrays),
        out_specs=[near] * len(shapes),
        out_shape=shapes,
        scratch_shapes=scratch,
        compiler_params=pltpu.CompilerParams(vmem_limit_bytes=VMEM_LIMIT),
        cost_estimate=pl.CostEstimate(
            flops=COST * members * size * width * (depth + variables),
            bytes_accessed=0,
            transcendentals=0,
        ),
        name="forward",
    )(*arrays)


def pair_tiles(own, others, targets, area, grad, start, unroll, first, loss_coef):
    members = own.shape[0]
    variables = own.shape[2]
    count = members * (1 + len(others))
    mine = members * TILE
    spots = [pl.multiple_of(start + u * TILE, TILE) for u in range(unroll)]
    ones = jnp.ones((8, 2 * variables), BF16)
    i = lax.broadcasted_iota(jnp.int32, (mine, count * TILE), 0)
    j = lax.broadcasted_iota(jnp.int32, (mine, count * TILE), 1)
    pair = jnp.logical_and(jnp.bitwise_and(i ^ j, TILE - 1) == 0, i != j)
    fulls, dists, weights = [], [], []
    for row in spots:
        rows = pl.ds(row, TILE)
        low = own[:, rows, :].reshape(mine, variables)
        full = jnp.concatenate(
            [low] + [o[:, rows, :].reshape(mine, variables) for o in others], axis=0
        )
        wide = full.astype(F32)
        square = wide * wide
        square_high = square.astype(BF16)
        square_low = (square - square_high.astype(F32)).astype(BF16)
        norms = nt(ones, jnp.concatenate([square_high, square_low], axis=1))[0:1, :] + EPSILON
        own_norms = jnp.sum(square[:mine], axis=1, keepdims=True)
        fulls.append(full)
        dists.append(jnp.maximum((own_norms + norms) - nt(low + low, full), EPSILON))
    for dist in dists:
        weight = jnp.where(pair, lax.rsqrt(dist), 0.0)
        total = jnp.sum(weight, axis=1, keepdims=True)
        weight_high = weight.astype(BF16)
        weight_low = (weight - weight_high.astype(F32)).astype(BF16)
        weights.append((total, jnp.concatenate([weight_high, weight_low], axis=0)))
    boths = [
        jnp.dot(weight, full, preferred_element_type=F32)
        for (_, weight), full in zip(weights, fulls)
    ]
    for row, full, both, (total, _) in zip(spots, fulls, boths, weights):
        mine_wide = full[:mine].astype(F32)
        weighted = both[:mine] + both[mine:]
        place = pl.ds(first + row, TILE)
        target = jnp.concatenate([targets[place, :]] * members, axis=0)
        scale = jnp.concatenate([area[place, :]] * members, axis=0)
        to_target = mine_wide - target
        spread = lax.rsqrt(jnp.sum(to_target * to_target, axis=1, keepdims=True) + EPSILON)
        pair_term = mine_wide * total - weighted
        value = scale * (
            to_target * (spread * (loss_coef / count)) - pair_term * (loss_coef / (count * (count - 1)))
        )
        grad[:, pl.ds(row, TILE), :] = value.astype(BF16).reshape(members, TILE, variables)


def backward_body(n_others, n_after, first, loss_coef, has_total, unroll, sub, dests, *refs):
    own, *refs = refs
    others, refs = refs[:n_others], refs[n_others:]
    targets, area, hidden, slope, latents, weight_out, *refs = refs
    if has_total:
        in_prior, out_prior, bias_prior, *refs = refs
    refs = refs[n_after:]
    if dests:
        keep, send, *refs = refs
    else:
        in_total, out_total, bias_total, *refs = refs
    grad, low = refs
    members, size, variables = own.shape

    @pl.loop(0, size // TILE // unroll)
    def _(t):
        pair_tiles(own, others, targets, area, grad, t * (unroll * TILE), unroll, first, loss_coef)

    w_out = weight_out[...]
    width = w_out.shape[0]
    bias_sum = bias_prior[...] if has_total else jnp.zeros((TILE, width), F32)
    for m in range(members):
        for r in range(size // sub):
            rows = pl.ds(r * sub, sub)
            pre = nt(grad[m, rows, :], w_out) * slope[m, rows, :]
            bias_sum += jnp.sum(pre.reshape(sub // TILE, TILE, width), axis=0)
            low[m, rows, :] = pre.astype(BF16)
    flat = lambda ref: ref[...].reshape(members * size, ref.shape[2])
    out_sum = tn(flat(hidden), flat(grad))
    depth = latents.shape[2]
    near = latents[:, pl.ds(first, size), :].reshape(members * size, depth)
    in_sum = tn(near, flat(low))
    if has_total:
        out_sum += out_prior[...]
        in_sum += in_prior[...]
    if not dests:
        in_total[...] = in_sum
        out_total[...] = out_sum
        bias_total[...] = bias_sum
        return
    core = lax.axis_index("mem") & 1
    share = in_sum.shape[0] // dests
    lanes = out_sum.shape[1]
    groups = width // lanes
    for half in range(2):
        for place in range(dests // 2):
            dest = 2 * place + half
            rows = slice(dest * share, (dest + 1) * share)
            block = jnp.concatenate(
                [in_sum[rows, q * lanes : (q + 1) * lanes] for q in range(groups)]
                + [out_sum[rows, :]]
                + [bias_sum[:, dest * share // lanes * lanes : (dest * share // lanes + 1) * lanes]],
                axis=0,
            )

            @pl.when(core == half)
            def _():
                keep[place] = block

            @pl.when(core != half)
            def _():
                send[place] = block


def backward(own, others, targets, area, hidden, slope, latents, weight_out, prior, first, loss_coef, dests=0, after=None, unroll=8, sub=256):
    members, size, variables = own.shape
    depth = latents.shape[2]
    width = weight_out.shape[0]
    whole = pl.BlockSpec(memory_space=pltpu.VMEM)
    count = members * (1 + len(others))
    if dests:
        rows = depth // dests * (width // variables + 1) + TILE
        shapes = [jax.ShapeDtypeStruct((dests // 2, rows, variables), F32)] * 2
    else:
        shapes = [
            jax.ShapeDtypeStruct((depth, width), F32),
            jax.ShapeDtypeStruct((width, variables), F32),
            jax.ShapeDtypeStruct((TILE, width), F32),
        ]
    return pl.pallas_call(
        partial(backward_body, len(others), 0 if after is None else 1, first, loss_coef, prior is not None, min(unroll, size // TILE), min(sub, size), dests),
        in_specs=[whole] * (3 + len(others))
        + [whole] * 4
        + ([whole] * 3 if prior is not None else [])
        + ([pl.BlockSpec(memory_space=pl.ANY)] if after is not None else []),
        out_specs=[whole] * len(shapes),
        out_shape=shapes,
        scratch_shapes=[
            pltpu.VMEM((members, size, variables), BF16),
            pltpu.VMEM((members, size, width), BF16),
        ],
        compiler_params=pltpu.CompilerParams(vmem_limit_bytes=VMEM_LIMIT),
        cost_estimate=pl.CostEstimate(
            flops=COST * members * size * (width * (depth + 2 * variables) + count * TILE * variables * 3),
            bytes_accessed=0,
            transcendentals=0,
        ),
        name="backward",
    )(own, *others, targets, area, hidden, slope, latents, weight_out, *(prior or ()), *(() if after is None else (after,)))


OFFSETS = ((2, 1), (3, 1), (2, 0), (3, 0), (1, 1), (1, 0), (0, 1))


def spread_body(keep, arrived, mine, *parts):
    z, x = lax.axis_index("pts"), lax.axis_index("mem") >> 1
    here = z * 2 + x
    mine[...] = keep[here] + arrived[here]
    for part, (dz, dx) in zip(parts, OFFSETS):
        there = (z ^ dz) * 2 + (x ^ dx)
        part[...] = (keep[there] + arrived[there]).astype(part.dtype)


def spread_out(keep, arrived, dtype):
    _, rows, lanes = keep.shape
    whole = pl.BlockSpec(memory_space=pltpu.VMEM)
    return pl.pallas_call(
        spread_body,
        in_specs=[whole, whole],
        out_specs=[whole] * (1 + len(OFFSETS)),
        out_shape=[jax.ShapeDtypeStruct((rows, lanes), F32)]
        + [jax.ShapeDtypeStruct((rows, lanes), dtype)] * len(OFFSETS),
        compiler_params=pltpu.CompilerParams(vmem_limit_bytes=SMALL_LIMIT),
        name="spread_out",
    )(keep, arrived)


def finish_body(share, mine, *refs):
    parts, (in_share, out_share, bias_share) = refs[:-3], refs[-3:]
    total = mine[...]
    for part in parts:
        total += part[...].astype(F32)
    lanes = total.shape[1]
    groups = in_share.shape[1] // lanes
    for q in range(groups):
        in_share[:, q * lanes : (q + 1) * lanes] = total[q * share : (q + 1) * share]
    out_share[...] = total[groups * share : (groups + 1) * share]
    row = jnp.sum(total[(groups + 1) * share :], axis=0, keepdims=True)
    place = lax.axis_index("mem")
    picked = row[:, :share]
    for k in range(1, lanes // share):
        picked = jnp.where(place == k, row[:, k * share : (k + 1) * share], picked)
    bias_share[...] = picked


def finish(mine, parts, share, width):
    lanes = mine.shape[1]
    whole = pl.BlockSpec(memory_space=pltpu.VMEM)
    return pl.pallas_call(
        partial(finish_body, share),
        in_specs=[whole] * (1 + len(parts)),
        out_specs=[whole] * 3,
        out_shape=[
            jax.ShapeDtypeStruct((share, width), F32),
            jax.ShapeDtypeStruct((share, lanes), F32),
            jax.ShapeDtypeStruct((1, share), F32),
        ],
        compiler_params=pltpu.CompilerParams(vmem_limit_bytes=SMALL_LIMIT),
        name="finish",
    )(mine, *parts)


def tie_body(value, after, tied):
    pass


def tie(value, after):
    anywhere = pl.BlockSpec(memory_space=pl.ANY)
    return pl.pallas_call(
        tie_body,
        in_specs=[anywhere] * 2,
        out_specs=anywhere,
        out_shape=jax.ShapeDtypeStruct(value.shape, value.dtype),
        input_output_aliases={0: 0},
        compiler_params=pltpu.CompilerParams(vmem_limit_bytes=TINY_LIMIT),
        name="tie",
    )(value, after)


def area_of(lat_row, rows_total):
    return jnp.cos(jnp.pi * (lat_row.astype(F32) + 0.5) / rows_total - jnp.pi / 2)


def swap_members(block, bit):
    size = lax.axis_size("mem")
    return lax.ppermute(block, "mem", [(i, i ^ bit) for i in range(size)])


def swap_points(block, dz, dx):
    points, members = lax.axis_size("pts"), lax.axis_size("mem")
    pairs = [
        (z * members + m, (z ^ dz) * members + (m ^ (2 * dx)))
        for z in range(points)
        for m in range(members)
    ]
    return lax.ppermute(block, ("pts", "mem"), pairs)


CHUNKS = (256, 256, 256, 256)


def chunks_of(points):
    scale = points // sum(CHUNKS)
    first = 0
    for size in CHUNKS:
        yield first, size * scale
        first += size * scale


def local(latents, member_seeds, targets, lat_row, weight_in, bias_in, weight_out):
    points = latents.shape[1]
    depth = latents.shape[2]
    width, variables = weight_out.shape
    devices_pts, devices_mem = lax.axis_size("pts"), lax.axis_size("mem")
    dests = devices_pts * devices_mem
    loss_coef = LOSS_SCALE / math.sqrt(points * devices_pts)
    area = jnp.broadcast_to(area_of(lat_row, LAT_ROWS)[:, None], (points, variables))
    packed = dests == 16 and devices_mem == 4
    plan = list(chunks_of(points))
    bits = [1 << k for k in reversed(range(devices_mem.bit_length() - 1))]
    saved = []
    arrays = [member_seeds, bias_in[None, :], latents, weight_in, weight_out]
    for first, size in plan:
        out, hidden, slope, *staged = forward(arrays, first, size, stage=first == 0)
        arrays = staged or arrays
        saved.append([[out, swap_members(out, bits[0])], hidden, slope])
    total = None
    sums = []
    for k, (first, size) in enumerate(plan):
        held, hidden, slope = saved[k]
        if k > LAG:
            held[1] = tie(held[1], sums[k - LAG - 1])
        for bit in bits[1:]:
            held = held + [swap_members(v, bit) for v in held]
        last = first + size == points
        total = list(backward(
            held[0], held[1:], targets, area, hidden, slope, arrays[1], arrays[3], total,
            first, loss_coef, dests if last and packed else 0,
            after=saved[-1][0][0] if k == 0 else None,
        ))
        sums.append(total[-1])
    if not packed:
        scatter = lambda v: lax.psum_scatter(v, ("pts", "mem"), scatter_dimension=0, tiled=True)
        return scatter(total[0]), scatter(total[1]), scatter(jnp.sum(total[2], axis=0))
    keep, send = total
    arrived = swap_members(send, 1)
    mine, *parts = spread_out(keep, arrived, LINK)
    parts = [swap_points(part, dz, dx) for part, (dz, dx) in zip(parts, OFFSETS)]
    in_share, out_share, bias_share = finish(mine, parts, depth // dests, width)
    return in_share, out_share, bias_share.reshape(depth // dests)


def solution(mesh):
    return jax.shard_map(
        local,
        mesh=mesh,
        in_specs=(
            P("mem", ("groups", "pts"), None),
            P(("groups", "mem")),
            P(("groups", "pts"), None),
            P(("groups", "pts")),
            P(),
            P(),
            P(),
        ),
        out_specs=(
            P(("groups", "pts", "mem"), None),
            P(("groups", "pts", "mem"), None),
            P(("groups", "pts", "mem")),
        ),
        check_vma=False,
    )
```

```python
from functools import partial
import math

import jax
import jax.numpy as jnp
from jax import lax
from jax.experimental import pallas as pl
from jax.experimental.pallas import tpu as pltpu
from jax.sharding import PartitionSpec as P

LAT_ROWS = 640
LOSS_SCALE = 256
EPSILON = 0.0001
TILE = 16
F32 = jnp.float32
BF16 = jnp.bfloat16
VMEM_LIMIT = 16 * 1024 * 1024
SMALL_LIMIT = 8 * 1024 * 1024
TINY_LIMIT = 1024 * 1024
LINK = BF16
COST = 2
LAG = 1
GELU_A = math.sqrt(2.0 / math.pi)
GELU_B = GELU_A * 0.044715


def nt(a, b):
    return lax.dot_general(a, b, (((1,), (1,)), ((), ())), preferred_element_type=F32)


def tn(a, b):
    return lax.dot_general(a, b, (((0,), (0,)), ((), ())), preferred_element_type=F32)


def in_hbm(v):
    return pltpu.with_memory_space_constraint(v, pltpu.HBM)


def piece_of(size, most):
    return max(k for k in range(TILE, most + 1, TILE) if size % k == 0)


def noise_row(seed, width):
    channel = lax.broadcasted_iota(jnp.int32, (1, width), 1)
    mixed = seed * (37 * channel + 11) + 7 * channel
    quotient = (mixed.astype(F32) * (1.0 / 65521.0)).astype(jnp.int32)
    rest = mixed - quotient * 65521
    rest = jnp.where(rest < 0, rest + 65521, rest)
    rest = jnp.where(rest >= 65521, rest - 65521, rest)
    return (rest.astype(F32) / 65521.0 - 0.5) * 2.0


def forward_body(first, size, sub, stage, *refs):
    if stage:
        seeds_in, bias_in, latents, w_in_ref, w_out_ref, *refs = refs
        outputs, hidden, slope, shift, latents_near, w_in_near, w_out_near, seeds, bias, sems = refs
        members, points = latents.shape[:2]
        loads = [
            (latents.at[m, pl.ds(first, size), :], latents_near.at[m, pl.ds(first, size), :])
            for m in range(members)
        ]
        loads[1:1] = [(bias_in, bias), (w_out_ref, w_out_near)]
        loads[0:0] = [(w_in_ref, w_in_near), (seeds_in, seeds)]
        if size < points:
            rest = pl.ds(size, points - size)
            loads.append((latents.at[:, rest, :], latents_near.at[:, rest, :]))
        loads = [pltpu.make_async_copy(a, b, sems.at[k]) for k, (a, b) in enumerate(loads)]
        for load in loads:
            load.start()
        latents, w_in_ref, w_out_ref = latents_near, w_in_near, w_out_near
        loads[1].wait()
        loads[3].wait()
        for m in range(members):
            shift[m : m + 1, :] = bias[...] + noise_row(seeds[m], bias.shape[1])
        loads[0].wait()
        loads[4].wait()
    else:
        _, shift, latents, w_in_ref, w_out_ref, outputs, hidden, slope = refs
    members = latents.shape[0]
    w_in = w_in_ref[...]
    w_out = w_out_ref[...]
    ahead = None
    behind = None

    def activate(k, rows, x):
        x2 = x * x
        half = 0.5 * jnp.tanh(x * (GELU_A + GELU_B * x2)) + 0.5
        h = x * half
        low = h.astype(BF16)
        hidden[k, rows, :] = low
        slope[k, rows, :] = half + (h - h * half) * (2.0 * GELU_A + 6.0 * GELU_B * x2)
        return k, rows, low

    def finish(k, rows, low):
        outputs[k, rows, :] = jnp.dot(low, w_out, preferred_element_type=F32).astype(BF16)

    for k in range(members):
        if stage:
            loads[2 if k == 0 else 4 + k].wait()
        for r in range(size // sub):
            rows = pl.ds(r * sub, sub)
            x = jnp.dot(latents[k, pl.ds(first + r * sub, sub), :], w_in, preferred_element_type=F32) + shift[k : k + 1, :]
            if behind is not None:
                finish(*behind)
            behind = activate(*ahead) if ahead is not None else None
            ahead = (k, rows, x)
    if behind is not None:
        finish(*behind)
    finish(*activate(*ahead))
    if stage:
        for load in loads[4 + members :]:
            load.wait()


def forward(arrays, first, size, after=None, sub=256):
    stage = after is None
    latents, weight_in, weight_out = arrays[-3:]
    members, _, depth = latents.shape
    width, variables = weight_out.shape
    near = pl.BlockSpec(memory_space=pltpu.VMEM)
    far = pl.BlockSpec(memory_space=pltpu.HBM)
    anywhere = pl.BlockSpec(memory_space=pl.ANY)
    shapes = [
        jax.ShapeDtypeStruct((members, size, variables), BF16),
        jax.ShapeDtypeStruct((members, size, width), BF16),
        jax.ShapeDtypeStruct((members, size, width), F32),
    ]
    scratch = []
    if stage:
        arrays = [in_hbm(v) for v in arrays]
        shapes.append(jax.ShapeDtypeStruct((members, width), F32))
        shapes += [jax.ShapeDtypeStruct(v.shape, v.dtype) for v in (latents, weight_in, weight_out)]
        scratch = [
            pltpu.SMEM((members,), jnp.int32),
            pltpu.VMEM((1, width), F32),
            pltpu.SemaphoreType.DMA((members + 5,)),
        ]
    return pl.pallas_call(
        partial(forward_body, first, size, piece_of(size, sub), stage),
        in_specs=[far] * len(arrays) if stage else [anywhere] + [near] * len(arrays),
        out_specs=[near] * len(shapes),
        out_shape=shapes,
        scratch_shapes=scratch,
        compiler_params=pltpu.CompilerParams(vmem_limit_bytes=VMEM_LIMIT),
        cost_estimate=pl.CostEstimate(
            flops=COST * members * size * width * (depth + variables),
            bytes_accessed=0,
            transcendentals=0,
        ),
        name="forward",
    )(*arrays if stage else (after, *arrays))


def pair_tiles(own, others, targets, area, grad, start, unroll, first, loss_coef):
    members = own.shape[0]
    variables = own.shape[2]
    count = members * (1 + len(others))
    mine = members * TILE
    spots = [pl.multiple_of(start + u * TILE, TILE) for u in range(unroll)]
    ones = jnp.ones((8, 2 * variables), BF16)
    i = lax.broadcasted_iota(jnp.int32, (mine, count * TILE), 0)
    j = lax.broadcasted_iota(jnp.int32, (mine, count * TILE), 1)
    pair = jnp.logical_and(jnp.bitwise_and(i ^ j, TILE - 1) == 0, i != j)
    fulls, dists, weights = [], [], []
    for row in spots:
        rows = pl.ds(row, TILE)
        low = own[:, rows, :].reshape(mine, variables)
        full = jnp.concatenate(
            [low] + [o[:, rows, :].reshape(mine, variables) for o in others], axis=0
        )
        wide = full.astype(F32)
        square = wide * wide
        square_high = square.astype(BF16)
        square_low = (square - square_high.astype(F32)).astype(BF16)
        norms = nt(ones, jnp.concatenate([square_high, square_low], axis=1))[0:1, :] + EPSILON
        own_norms = jnp.sum(square[:mine], axis=1, keepdims=True)
        fulls.append(full)
        dists.append(jnp.maximum((own_norms + norms) - nt(low + low, full), EPSILON))
    for dist in dists:
        weight = jnp.where(pair, lax.rsqrt(dist), 0.0)
        total = jnp.sum(weight, axis=1, keepdims=True)
        weight_high = weight.astype(BF16)
        weight_low = (weight - weight_high.astype(F32)).astype(BF16)
        weights.append((total, jnp.concatenate([weight_high, weight_low], axis=0)))
    boths = [
        jnp.dot(weight, full, preferred_element_type=F32)
        for (_, weight), full in zip(weights, fulls)
    ]
    for row, full, both, (total, _) in zip(spots, fulls, boths, weights):
        mine_wide = full[:mine].astype(F32)
        weighted = both[:mine] + both[mine:]
        place = pl.ds(first + row, TILE)
        target = jnp.concatenate([targets[place, :]] * members, axis=0)
        scale = jnp.concatenate([area[place, :]] * members, axis=0)
        to_target = mine_wide - target
        spread = lax.rsqrt(jnp.sum(to_target * to_target, axis=1, keepdims=True) + EPSILON)
        pair_term = mine_wide * total - weighted
        value = scale * (
            to_target * (spread * (loss_coef / count)) - pair_term * (loss_coef / (count * (count - 1)))
        )
        grad[:, pl.ds(row, TILE), :] = value.astype(BF16).reshape(members, TILE, variables)


def backward_body(n_others, n_after, first, loss_coef, has_total, unroll, sub, dests, *refs):
    own, *refs = refs
    others, refs = refs[:n_others], refs[n_others:]
    targets, area, hidden, slope, latents, weight_out, *refs = refs
    if has_total:
        in_prior, out_prior, bias_prior, *refs = refs
    refs = refs[n_after:]
    if dests:
        keep, send, *refs = refs
    else:
        in_total, out_total, bias_total, *refs = refs
    grad, low = refs
    members, size, variables = own.shape

    @pl.loop(0, size // TILE // unroll)
    def _(t):
        pair_tiles(own, others, targets, area, grad, t * (unroll * TILE), unroll, first, loss_coef)

    w_out = weight_out[...]
    width = w_out.shape[0]
    bias_sum = bias_prior[...] if has_total else jnp.zeros((TILE, width), F32)
    for m in range(members):
        for r in range(size // sub):
            rows = pl.ds(r * sub, sub)
            pre = nt(grad[m, rows, :], w_out) * slope[m, rows, :]
            bias_sum += jnp.sum(pre.reshape(sub // TILE, TILE, width), axis=0)
            low[m, rows, :] = pre.astype(BF16)
    flat = lambda ref: ref[...].reshape(members * size, ref.shape[2])
    out_sum = tn(flat(hidden), flat(grad))
    depth = latents.shape[2]
    near = latents[:, pl.ds(first, size), :].reshape(members * size, depth)
    in_sum = tn(near, flat(low))
    if has_total:
        out_sum += out_prior[...]
        in_sum += in_prior[...]
    if not dests:
        in_total[...] = in_sum
        out_total[...] = out_sum
        bias_total[...] = bias_sum
        return
    core = lax.axis_index("mem") & 1
    share = in_sum.shape[0] // dests
    lanes = out_sum.shape[1]
    groups = width // lanes
    for half in range(2):
        for place in range(dests // 2):
            dest = 2 * place + half
            rows = slice(dest * share, (dest + 1) * share)
            block = jnp.concatenate(
                [in_sum[rows, q * lanes : (q + 1) * lanes] for q in range(groups)]
                + [out_sum[rows, :]]
                + [bias_sum[:, dest * share // lanes * lanes : (dest * share // lanes + 1) * lanes]],
                axis=0,
            )

            @pl.when(core == half)
            def _():
                keep[place] = block

            @pl.when(core != half)
            def _():
                send[place] = block


def backward(own, others, targets, area, hidden, slope, latents, weight_out, prior, first, loss_coef, dests=0, after=None, unroll=8, sub=256):
    members, size, variables = own.shape
    depth = latents.shape[2]
    width = weight_out.shape[0]
    whole = pl.BlockSpec(memory_space=pltpu.VMEM)
    count = members * (1 + len(others))
    if dests:
        rows = depth // dests * (width // variables + 1) + TILE
        shapes = [jax.ShapeDtypeStruct((dests // 2, rows, variables), F32)] * 2
    else:
        shapes = [
            jax.ShapeDtypeStruct((depth, width), F32),
            jax.ShapeDtypeStruct((width, variables), F32),
            jax.ShapeDtypeStruct((TILE, width), F32),
        ]
    return pl.pallas_call(
        partial(backward_body, len(others), 0 if after is None else 1, first, loss_coef, prior is not None, math.gcd(unroll, size // TILE), piece_of(size, sub), dests),
        in_specs=[whole] * (3 + len(others))
        + [whole] * 4
        + ([whole] * 3 if prior is not None else [])
        + ([pl.BlockSpec(memory_space=pl.ANY)] if after is not None else []),
        out_specs=[whole] * len(shapes),
        out_shape=shapes,
        scratch_shapes=[
            pltpu.VMEM((members, size, variables), BF16),
            pltpu.VMEM((members, size, width), BF16),
        ],
        compiler_params=pltpu.CompilerParams(vmem_limit_bytes=VMEM_LIMIT),
        cost_estimate=pl.CostEstimate(
            flops=COST * members * size * (width * (depth + 2 * variables) + count * TILE * variables * 3),
            bytes_accessed=0,
            transcendentals=0,
        ),
        name="backward",
    )(own, *others, targets, area, hidden, slope, latents, weight_out, *(prior or ()), *(() if after is None else (after,)))


OFFSETS = ((2, 1), (3, 1), (2, 0), (3, 0), (1, 1), (1, 0), (0, 1))


def spread_body(keep, arrived, mine, *parts):
    z, x = lax.axis_index("pts"), lax.axis_index("mem") >> 1
    here = z * 2 + x
    mine[...] = keep[here] + arrived[here]
    for part, (dz, dx) in zip(parts, OFFSETS):
        there = (z ^ dz) * 2 + (x ^ dx)
        part[...] = (keep[there] + arrived[there]).astype(part.dtype)


def spread_out(keep, arrived, dtype):
    _, rows, lanes = keep.shape
    whole = pl.BlockSpec(memory_space=pltpu.VMEM)
    return pl.pallas_call(
        spread_body,
        in_specs=[whole, whole],
        out_specs=[whole] * (1 + len(OFFSETS)),
        out_shape=[jax.ShapeDtypeStruct((rows, lanes), F32)]
        + [jax.ShapeDtypeStruct((rows, lanes), dtype)] * len(OFFSETS),
        compiler_params=pltpu.CompilerParams(vmem_limit_bytes=SMALL_LIMIT),
        name="spread_out",
    )(keep, arrived)


def finish_body(share, mine, *refs):
    parts, (in_share, out_share, bias_share) = refs[:-3], refs[-3:]
    total = mine[...]
    for part in parts:
        total += part[...].astype(F32)
    lanes = total.shape[1]
    groups = in_share.shape[1] // lanes
    for q in range(groups):
        in_share[:, q * lanes : (q + 1) * lanes] = total[q * share : (q + 1) * share]
    out_share[...] = total[groups * share : (groups + 1) * share]
    row = jnp.sum(total[(groups + 1) * share :], axis=0, keepdims=True)
    place = lax.axis_index("mem")
    picked = row[:, :share]
    for k in range(1, lanes // share):
        picked = jnp.where(place == k, row[:, k * share : (k + 1) * share], picked)
    bias_share[...] = picked


def finish(mine, parts, share, width):
    lanes = mine.shape[1]
    whole = pl.BlockSpec(memory_space=pltpu.VMEM)
    return pl.pallas_call(
        partial(finish_body, share),
        in_specs=[whole] * (1 + len(parts)),
        out_specs=[whole] * 3,
        out_shape=[
            jax.ShapeDtypeStruct((share, width), F32),
            jax.ShapeDtypeStruct((share, lanes), F32),
            jax.ShapeDtypeStruct((1, share), F32),
        ],
        compiler_params=pltpu.CompilerParams(vmem_limit_bytes=SMALL_LIMIT),
        name="finish",
    )(mine, *parts)


def tie_body(value, after, tied):
    pass


def tie(value, after):
    anywhere = pl.BlockSpec(memory_space=pl.ANY)
    return pl.pallas_call(
        tie_body,
        in_specs=[anywhere] * 2,
        out_specs=anywhere,
        out_shape=jax.ShapeDtypeStruct(value.shape, value.dtype),
        input_output_aliases={0: 0},
        compiler_params=pltpu.CompilerParams(vmem_limit_bytes=TINY_LIMIT),
        name="tie",
    )(value, after)


def area_of(lat_row, rows_total):
    return jnp.cos(jnp.pi * (lat_row.astype(F32) + 0.5) / rows_total - jnp.pi / 2)


def swap_members(block, bit):
    size = lax.axis_size("mem")
    return lax.ppermute(block, "mem", [(i, i ^ bit) for i in range(size)])


def swap_points(block, dz, dx):
    points, members = lax.axis_size("pts"), lax.axis_size("mem")
    pairs = [
        (z * members + m, (z ^ dz) * members + (m ^ (2 * dx)))
        for z in range(points)
        for m in range(members)
    ]
    return lax.ppermute(block, ("pts", "mem"), pairs)


CHUNKS = (256, 256, 256, 256)


def chunks_of(points):
    scale = points // sum(CHUNKS)
    first = 0
    for size in CHUNKS:
        yield first, size * scale
        first += size * scale


def local(latents, member_seeds, targets, lat_row, weight_in, bias_in, weight_out):
    points = latents.shape[1]
    depth = latents.shape[2]
    width, variables = weight_out.shape
    devices_pts, devices_mem = lax.axis_size("pts"), lax.axis_size("mem")
    dests = devices_pts * devices_mem
    loss_coef = LOSS_SCALE / math.sqrt(points * devices_pts)
    area = jnp.broadcast_to(area_of(lat_row, LAT_ROWS)[:, None], (points, variables))
    packed = dests == 16 and devices_mem == 4
    plan = list(chunks_of(points))
    bits = [1 << k for k in reversed(range(devices_mem.bit_length() - 1))]
    saved = []
    out = None
    arrays = [member_seeds, bias_in[None, :], latents, weight_in, weight_out]
    for first, size in plan:
        out, hidden, slope, *staged = forward(arrays, first, size, after=out)
        arrays = staged or arrays
        saved.append([[out, swap_members(out, bits[0])], hidden, slope])
    total = None
    sums = []
    for k, (first, size) in enumerate(plan):
        held, hidden, slope = saved[k]
        if k > LAG:
            held[1] = tie(held[1], sums[k - LAG - 1])
        for bit in bits[1:]:
            held = held + [swap_members(v, bit) for v in held]
        last = first + size == points
        total = list(backward(
            held[0], held[1:], targets, area, hidden, slope, arrays[1], arrays[3], total,
            first, loss_coef, dests if last and packed else 0,
            after=saved[-1][0][0] if k == 0 else None,
        ))
        sums.append(total[-1])
    if not packed:
        scatter = lambda v: lax.psum_scatter(v, ("pts", "mem"), scatter_dimension=0, tiled=True)
        return scatter(total[0]), scatter(total[1]), scatter(jnp.sum(total[2], axis=0))
    keep, send = total
    arrived = swap_members(send, 1)
    mine, *parts = spread_out(keep, arrived, LINK)
    parts = [swap_points(part, dz, dx) for part, (dz, dx) in zip(parts, OFFSETS)]
    in_share, out_share, bias_share = finish(mine, parts, depth // dests, width)
    return in_share, out_share, bias_share.reshape(depth // dests)


def solution(mesh):
    return jax.shard_map(
        local,
        mesh=mesh,
        in_specs=(
            P("mem", ("groups", "pts"), None),
            P(("groups", "mem")),
            P(("groups", "pts"), None),
            P(("groups", "pts")),
            P(),
            P(),
            P(),
        ),
        out_specs=(
            P(("groups", "pts", "mem"), None),
            P(("groups", "pts", "mem"), None),
            P(("groups", "pts", "mem")),
        ),
        check_vma=False,
    )
```

```python
from functools import partial
import math

import jax
import jax.numpy as jnp
from jax import lax
from jax.experimental import pallas as pl
from jax.experimental.pallas import tpu as pltpu
from jax.sharding import PartitionSpec as P

LAT_ROWS = 640
LOSS_SCALE = 256
EPSILON = 0.0001
TILE = 16
F32 = jnp.float32
BF16 = jnp.bfloat16
VMEM_LIMIT = 16 * 1024 * 1024
SMALL_LIMIT = 8 * 1024 * 1024
TINY_LIMIT = 1024 * 1024
LINK = BF16
LAST = BF16
COST_F = 2
COST_B = 2
LAGS = (9, 1, 1)
GELU_A = math.sqrt(2.0 / math.pi)
GELU_B = GELU_A * 0.044715


def nt(a, b):
    return lax.dot_general(a, b, (((1,), (1,)), ((), ())), preferred_element_type=F32)


def tn(a, b):
    return lax.dot_general(a, b, (((0,), (0,)), ((), ())), preferred_element_type=F32)


def in_hbm(v):
    return pltpu.with_memory_space_constraint(v, pltpu.HBM)


def piece_of(size, most):
    return max(k for k in range(TILE, most + 1, TILE) if size % k == 0)


def noise_row(seed, width):
    channel = lax.broadcasted_iota(jnp.int32, (1, width), 1)
    mixed = seed * (37 * channel + 11) + 7 * channel
    quotient = (mixed.astype(F32) * (1.0 / 65521.0)).astype(jnp.int32)
    rest = mixed - quotient * 65521
    rest = jnp.where(rest < 0, rest + 65521, rest)
    rest = jnp.where(rest >= 65521, rest - 65521, rest)
    return (rest.astype(F32) / 65521.0 - 0.5) * 2.0


def forward_body(first, size, sub, stage, *refs):
    if stage:
        seeds_in, bias_in, latents, w_in_ref, w_out_ref, *refs = refs
        outputs, hidden, slope, shift, latents_near, w_in_near, w_out_near, seeds, bias, sems = refs
        members, points = latents.shape[:2]
        loads = [
            (latents.at[m, pl.ds(first, size), :], latents_near.at[m, pl.ds(first, size), :])
            for m in range(members)
        ]
        loads[1:1] = [(bias_in, bias), (w_out_ref, w_out_near)]
        loads[0:0] = [(w_in_ref, w_in_near), (seeds_in, seeds)]
        if size < points:
            rest = pl.ds(size, points - size)
            loads.append((latents.at[:, rest, :], latents_near.at[:, rest, :]))
        loads = [pltpu.make_async_copy(a, b, sems.at[k]) for k, (a, b) in enumerate(loads)]
        for load in loads[: 4 + members]:
            load.start()
        latents, w_in_ref, w_out_ref = latents_near, w_in_near, w_out_near
        loads[1].wait()
        loads[3].wait()
        for m in range(members):
            shift[m : m + 1, :] = bias[...] + noise_row(seeds[m], bias.shape[1])
        loads[0].wait()
        loads[4].wait()
        for load in loads[4 + members :]:
            load.start()
    else:
        _, shift, latents, w_in_ref, w_out_ref, outputs, hidden, slope = refs
    members = latents.shape[0]
    w_in = w_in_ref[...]
    w_out = w_out_ref[...]
    ahead = None
    behind = None

    def activate(k, rows, x):
        x2 = x * x
        half = 0.5 * jnp.tanh(x * (GELU_A + GELU_B * x2)) + 0.5
        h = x * half
        low = h.astype(BF16)
        hidden[k, rows, :] = low
        slope[k, rows, :] = half + (h - h * half) * (2.0 * GELU_A + 6.0 * GELU_B * x2)
        return k, rows, low

    def finish(k, rows, low):
        outputs[k, rows, :] = jnp.dot(low, w_out, preferred_element_type=F32).astype(BF16)

    for k in range(members):
        if stage:
            loads[2 if k == 0 else 4 + k].wait()
        for r in range(size // sub):
            rows = pl.ds(r * sub, sub)
            x = jnp.dot(latents[k, pl.ds(first + r * sub, sub), :], w_in, preferred_element_type=F32) + shift[k : k + 1, :]
            if behind is not None:
                finish(*behind)
            behind = activate(*ahead) if ahead is not None else None
            ahead = (k, rows, x)
    if behind is not None:
        finish(*behind)
    finish(*activate(*ahead))
    if stage:
        for load in loads[4 + members :]:
            load.wait()


def forward(arrays, first, size, after=None, sub=256):
    stage = after is None
    latents, weight_in, weight_out = arrays[-3:]
    members, _, depth = latents.shape
    width, variables = weight_out.shape
    near = pl.BlockSpec(memory_space=pltpu.VMEM)
    far = pl.BlockSpec(memory_space=pltpu.HBM)
    anywhere = pl.BlockSpec(memory_space=pl.ANY)
    shapes = [
        jax.ShapeDtypeStruct((members, size, variables), BF16),
        jax.ShapeDtypeStruct((members, size, width), BF16),
        jax.ShapeDtypeStruct((members, size, width), F32),
    ]
    scratch = []
    if stage:
        arrays = [in_hbm(v) for v in arrays]
        shapes.append(jax.ShapeDtypeStruct((members, width), F32))
        shapes += [jax.ShapeDtypeStruct(v.shape, v.dtype) for v in (latents, weight_in, weight_out)]
        scratch = [
            pltpu.SMEM((members,), jnp.int32),
            pltpu.VMEM((1, width), F32),
            pltpu.SemaphoreType.DMA((members + 5,)),
        ]
    return pl.pallas_call(
        partial(forward_body, first, size, piece_of(size, sub), stage),
        in_specs=[far] * len(arrays) if stage else [anywhere] + [near] * len(arrays),
        out_specs=[near] * len(shapes),
        out_shape=shapes,
        scratch_shapes=scratch,
        compiler_params=pltpu.CompilerParams(vmem_limit_bytes=VMEM_LIMIT),
        cost_estimate=pl.CostEstimate(
            flops=int(COST_F * members * size * width * (depth + variables)),
            bytes_accessed=0,
            transcendentals=0,
        ),
        name="forward",
    )(*arrays if stage else (after, *arrays))


def pair_tiles(own, others, targets, area, grad, start, unroll, first, loss_coef):
    members = own.shape[0]
    variables = own.shape[2]
    count = members * (1 + len(others))
    mine = members * TILE
    spots = [pl.multiple_of(start + u * TILE, TILE) for u in range(unroll)]
    ones = jnp.ones((8, 2 * variables), BF16)
    i = lax.broadcasted_iota(jnp.int32, (mine, count * TILE), 0)
    j = lax.broadcasted_iota(jnp.int32, (mine, count * TILE), 1)
    pair = jnp.logical_and(jnp.bitwise_and(i ^ j, TILE - 1) == 0, i != j)
    fulls, dists, weights = [], [], []
    for row in spots:
        rows = pl.ds(row, TILE)
        low = own[:, rows, :].reshape(mine, variables)
        full = jnp.concatenate(
            [low] + [o[:, rows, :].reshape(mine, variables) for o in others], axis=0
        )
        wide = full.astype(F32)
        square = wide * wide
        square_high = square.astype(BF16)
        square_low = (square - square_high.astype(F32)).astype(BF16)
        norms = nt(ones, jnp.concatenate([square_high, square_low], axis=1))[0:1, :] + EPSILON
        own_norms = jnp.sum(square[:mine], axis=1, keepdims=True)
        fulls.append(full)
        dists.append(jnp.maximum((own_norms + norms) - nt(low + low, full), EPSILON))
    for dist in dists:
        weight = jnp.where(pair, lax.rsqrt(dist), 0.0)
        total = jnp.sum(weight, axis=1, keepdims=True)
        weight_high = weight.astype(BF16)
        weight_low = (weight - weight_high.astype(F32)).astype(BF16)
        weights.append((total, jnp.concatenate([weight_high, weight_low], axis=0)))
    boths = [
        jnp.dot(weight, full, preferred_element_type=F32)
        for (_, weight), full in zip(weights, fulls)
    ]
    for row, full, both, (total, _) in zip(spots, fulls, boths, weights):
        mine_wide = full[:mine].astype(F32)
        weighted = both[:mine] + both[mine:]
        place = pl.ds(first + row, TILE)
        target = jnp.concatenate([targets[place, :]] * members, axis=0)
        scale = jnp.concatenate([area[place, :]] * members, axis=0)
        to_target = mine_wide - target
        spread = lax.rsqrt(jnp.sum(to_target * to_target, axis=1, keepdims=True) + EPSILON)
        pair_term = mine_wide * total - weighted
        value = scale * (
            to_target * (spread * (loss_coef / count)) - pair_term * (loss_coef / (count * (count - 1)))
        )
        grad[:, pl.ds(row, TILE), :] = value.astype(BF16).reshape(members, TILE, variables)


def backward_body(n_others, n_after, first, loss_coef, has_total, unroll, sub, dests, *refs):
    own, *refs = refs
    others, refs = refs[:n_others], refs[n_others:]
    targets, area, hidden, slope, latents, weight_out, *refs = refs
    if has_total:
        in_prior, out_prior, bias_prior, *refs = refs
    refs = refs[n_after:]
    if dests:
        keep, send, *refs = refs
    else:
        in_total, out_total, bias_total, *refs = refs
    grad, low = refs
    members, size, variables = own.shape

    @pl.loop(0, size // TILE // unroll)
    def _(t):
        pair_tiles(own, others, targets, area, grad, t * (unroll * TILE), unroll, first, loss_coef)

    w_out = weight_out[...]
    width = w_out.shape[0]
    bias_sum = bias_prior[...] if has_total else jnp.zeros((TILE, width), F32)
    for m in range(members):
        for r in range(size // sub):
            rows = pl.ds(r * sub, sub)
            pre = nt(grad[m, rows, :], w_out) * slope[m, rows, :]
            bias_sum += jnp.sum(pre.reshape(sub // TILE, TILE, width), axis=0)
            low[m, rows, :] = pre.astype(BF16)
    flat = lambda ref: ref[...].reshape(members * size, ref.shape[2])
    out_sum = tn(flat(hidden), flat(grad))
    depth = latents.shape[2]
    near = latents[:, pl.ds(first, size), :].reshape(members * size, depth)
    in_sum = tn(near, flat(low))
    if has_total:
        out_sum += out_prior[...]
        in_sum += in_prior[...]
    if not dests:
        in_total[...] = in_sum
        out_total[...] = out_sum
        bias_total[...] = bias_sum
        return
    core = lax.axis_index("mem") & 1
    share = in_sum.shape[0] // dests
    lanes = out_sum.shape[1]
    groups = width // lanes
    for half in range(2):
        for place in range(dests // 2):
            dest = 2 * place + half
            rows = slice(dest * share, (dest + 1) * share)
            block = jnp.concatenate(
                [in_sum[rows, q * lanes : (q + 1) * lanes] for q in range(groups)]
                + [out_sum[rows, :]]
                + [bias_sum[:, dest * share // lanes * lanes : (dest * share // lanes + 1) * lanes]],
                axis=0,
            )

            @pl.when(core == half)
            def _():
                keep[place] = block

            @pl.when(core != half)
            def _():
                send[place] = block


def backward(own, others, targets, area, hidden, slope, latents, weight_out, prior, first, loss_coef, dests=0, after=None, unroll=8, sub=256):
    members, size, variables = own.shape
    depth = latents.shape[2]
    width = weight_out.shape[0]
    whole = pl.BlockSpec(memory_space=pltpu.VMEM)
    count = members * (1 + len(others))
    if dests:
        rows = depth // dests * (width // variables + 1) + TILE
        shapes = [jax.ShapeDtypeStruct((dests // 2, rows, variables), F32)] * 2
    else:
        shapes = [
            jax.ShapeDtypeStruct((depth, width), F32),
            jax.ShapeDtypeStruct((width, variables), F32),
            jax.ShapeDtypeStruct((TILE, width), F32),
        ]
    return pl.pallas_call(
        partial(backward_body, len(others), 0 if after is None else 1, first, loss_coef, prior is not None, math.gcd(unroll, size // TILE), piece_of(size, sub), dests),
        in_specs=[whole] * (3 + len(others))
        + [whole] * 4
        + ([whole] * 3 if prior is not None else [])
        + ([pl.BlockSpec(memory_space=pl.ANY)] if after is not None else []),
        out_specs=[whole] * len(shapes),
        out_shape=shapes,
        scratch_shapes=[
            pltpu.VMEM((members, size, variables), BF16),
            pltpu.VMEM((members, size, width), BF16),
        ],
        compiler_params=pltpu.CompilerParams(vmem_limit_bytes=VMEM_LIMIT),
        cost_estimate=pl.CostEstimate(
            flops=int(COST_B * members * size * (width * (depth + 2 * variables) + count * TILE * variables * 3)),
            bytes_accessed=0,
            transcendentals=0,
        ),
        name="backward",
    )(own, *others, targets, area, hidden, slope, latents, weight_out, *(prior or ()), *(() if after is None else (after,)))


SQUARE = ((1, 1), (1, 0), (0, 1))


def spread_body(keep, arrived, mine, *parts):
    z, x = lax.axis_index("pts") & 1, lax.axis_index("mem") >> 1
    for high in range(2):
        here = (2 * high + z) * 2 + x
        mine[high] = keep[here] + arrived[here]
        for part, (dz, dx) in zip(parts, SQUARE):
            there = (2 * high + (z ^ dz)) * 2 + (x ^ dx)
            part[high] = (keep[there] + arrived[there]).astype(part.dtype)


def spread_out(keep, arrived):
    _, rows, lanes = keep.shape
    whole = pl.BlockSpec(memory_space=pltpu.VMEM)
    return pl.pallas_call(
        spread_body,
        in_specs=[whole, whole],
        out_specs=[whole] * (1 + len(SQUARE)),
        out_shape=[jax.ShapeDtypeStruct((2, rows, lanes), F32)]
        + [jax.ShapeDtypeStruct((2, rows, lanes), LINK)] * len(SQUARE),
        compiler_params=pltpu.CompilerParams(vmem_limit_bytes=SMALL_LIMIT),
        name="spread_out",
    )(keep, arrived)


def fold_body(mine, *refs):
    parts, (keep, send) = refs[:-2], refs[-2:]
    high = lax.axis_index("pts") >> 1
    for place, out in ((high, keep), (1 - high, send)):
        total = mine[place]
        for part in parts:
            total += part[place].astype(F32)
        out[...] = total.astype(out.dtype)


def fold(mine, parts):
    _, rows, lanes = mine.shape
    whole = pl.BlockSpec(memory_space=pltpu.VMEM)
    return pl.pallas_call(
        fold_body,
        in_specs=[whole] * (1 + len(parts)),
        out_specs=[whole] * 2,
        out_shape=[
            jax.ShapeDtypeStruct((rows, lanes), F32),
            jax.ShapeDtypeStruct((rows, lanes), LAST),
        ],
        compiler_params=pltpu.CompilerParams(vmem_limit_bytes=SMALL_LIMIT),
        name="fold",
    )(mine, *parts)


def finish_body(share, mine, *refs):
    parts, (in_share, out_share, bias_share) = refs[:-3], refs[-3:]
    total = mine[...]
    for part in parts:
        total += part[...].astype(F32)
    lanes = total.shape[1]
    groups = in_share.shape[1] // lanes
    for q in range(groups):
        in_share[:, q * lanes : (q + 1) * lanes] = total[q * share : (q + 1) * share]
    out_share[...] = total[groups * share : (groups + 1) * share]
    row = jnp.sum(total[(groups + 1) * share :], axis=0, keepdims=True)
    place = lax.axis_index("mem")
    picked = row[:, :share]
    for k in range(1, lanes // share):
        picked = jnp.where(place == k, row[:, k * share : (k + 1) * share], picked)
    bias_share[...] = picked


def finish(mine, parts, share, width):
    lanes = mine.shape[1]
    whole = pl.BlockSpec(memory_space=pltpu.VMEM)
    return pl.pallas_call(
        partial(finish_body, share),
        in_specs=[whole] * (1 + len(parts)),
        out_specs=[whole] * 3,
        out_shape=[
            jax.ShapeDtypeStruct((share, width), F32),
            jax.ShapeDtypeStruct((share, lanes), F32),
            jax.ShapeDtypeStruct((1, share), F32),
        ],
        compiler_params=pltpu.CompilerParams(vmem_limit_bytes=SMALL_LIMIT),
        name="finish",
    )(mine, *parts)


def tie_body(value, after, tied):
    pass


def tie(value, after):
    anywhere = pl.BlockSpec(memory_space=pl.ANY)
    return pl.pallas_call(
        tie_body,
        in_specs=[anywhere] * 2,
        out_specs=anywhere,
        out_shape=jax.ShapeDtypeStruct(value.shape, value.dtype),
        input_output_aliases={0: 0},
        compiler_params=pltpu.CompilerParams(vmem_limit_bytes=TINY_LIMIT),
        name="tie",
    )(value, after)


def area_of(lat_row, rows_total):
    return jnp.cos(jnp.pi * (lat_row.astype(F32) + 0.5) / rows_total - jnp.pi / 2)


def swap_members(block, bit):
    size = lax.axis_size("mem")
    return lax.ppermute(block, "mem", [(i, i ^ bit) for i in range(size)])


def swap_points(block, dz, dx):
    points, members = lax.axis_size("pts"), lax.axis_size("mem")
    pairs = [
        (z * members + m, (z ^ dz) * members + (m ^ (2 * dx)))
        for z in range(points)
        for m in range(members)
    ]
    return lax.ppermute(block, ("pts", "mem"), pairs)


CHUNKS = (256, 256, 256, 256)


def chunks_of(points):
    scale = points // sum(CHUNKS)
    first = 0
    for size in CHUNKS:
        yield first, size * scale
        first += size * scale


def local(latents, member_seeds, targets, lat_row, weight_in, bias_in, weight_out):
    points = latents.shape[1]
    depth = latents.shape[2]
    width, variables = weight_out.shape
    devices_pts, devices_mem = lax.axis_size("pts"), lax.axis_size("mem")
    dests = devices_pts * devices_mem
    loss_coef = LOSS_SCALE / math.sqrt(points * devices_pts)
    area = jnp.broadcast_to(area_of(lat_row, LAT_ROWS)[:, None], (points, variables))
    packed = dests == 16 and devices_mem == 4
    plan = list(chunks_of(points))
    bits = [1 << k for k in reversed(range(devices_mem.bit_length() - 1))]
    saved = []
    out = None
    arrays = [member_seeds, bias_in[None, :], latents, weight_in, weight_out]
    for first, size in plan:
        out, hidden, slope, *staged = forward(arrays, first, size, after=out)
        arrays = staged or arrays
        saved.append([[out, swap_members(out, bits[0])], hidden, slope])
    total = None
    sums = []
    for k, (first, size) in enumerate(plan):
        held, hidden, slope = saved[k]
        if k and LAGS[k - 1] < k:
            held[1] = tie(held[1], sums[k - 1 - LAGS[k - 1]])
        for bit in bits[1:]:
            held = held + [swap_members(v, bit) for v in held]
        last = first + size == points
        total = list(backward(
            held[0], held[1:], targets, area, hidden, slope, arrays[1], arrays[3], total,
            first, loss_coef, dests if last and packed else 0,
            after=saved[-1][0][0] if k == 0 else None,
        ))
        sums.append(total[-1])
    if not packed:
        scatter = lambda v: lax.psum_scatter(v, ("pts", "mem"), scatter_dimension=0, tiled=True)
        return scatter(total[0]), scatter(total[1]), scatter(jnp.sum(total[2], axis=0))
    keep, send = total
    arrived = swap_members(send, 1)
    mine, *parts = spread_out(keep, arrived)
    parts = [swap_points(part, dz, dx) for part, (dz, dx) in zip(parts, SQUARE)]
    keep, send = fold(mine, parts)
    in_share, out_share, bias_share = finish(keep, [swap_points(send, 2, 0)], depth // dests, width)
    return in_share, out_share, bias_share.reshape(depth // dests)


def solution(mesh):
    return jax.shard_map(
        local,
        mesh=mesh,
        in_specs=(
            P("mem", ("groups", "pts"), None),
            P(("groups", "mem")),
            P(("groups", "pts"), None),
            P(("groups", "pts")),
            P(),
            P(),
            P(),
        ),
        out_specs=(
            P(("groups", "pts", "mem"), None),
            P(("groups", "pts", "mem"), None),
            P(("groups", "pts", "mem")),
        ),
        check_vma=False,
    )
```

```python
from functools import partial
import math

import jax
import jax.numpy as jnp
from jax import lax
from jax.experimental import pallas as pl
from jax.experimental.pallas import tpu as pltpu
from jax.sharding import PartitionSpec as P

LAT_ROWS = 640
LOSS_SCALE = 256
EPSILON = 0.0001
TILE = 16
F32 = jnp.float32
BF16 = jnp.bfloat16
VMEM_LIMIT = 16 * 1024 * 1024
SMALL_LIMIT = 8 * 1024 * 1024
TINY_LIMIT = 1024 * 1024
LINK = BF16
COST_F = 2
COST_B = 8
LAGS = (1, 1, 1)
GELU_A = math.sqrt(2.0 / math.pi)
GELU_B = GELU_A * 0.044715


def nt(a, b):
    return lax.dot_general(a, b, (((1,), (1,)), ((), ())), preferred_element_type=F32)


def tn(a, b):
    return lax.dot_general(a, b, (((0,), (0,)), ((), ())), preferred_element_type=F32)


def in_hbm(v):
    return pltpu.with_memory_space_constraint(v, pltpu.HBM)


def piece_of(size, most):
    return max(k for k in range(TILE, most + 1, TILE) if size % k == 0)


def noise_row(seed, width):
    channel = lax.broadcasted_iota(jnp.int32, (1, width), 1)
    mixed = seed * (37 * channel + 11) + 7 * channel
    quotient = (mixed.astype(F32) * (1.0 / 65521.0)).astype(jnp.int32)
    rest = mixed - quotient * 65521
    rest = jnp.where(rest < 0, rest + 65521, rest)
    rest = jnp.where(rest >= 65521, rest - 65521, rest)
    return (rest.astype(F32) / 65521.0 - 0.5) * 2.0


def forward_body(first, size, sub, stage, *refs):
    if stage:
        seeds_in, bias_in, latents, w_in_ref, w_out_ref, *refs = refs
        outputs, hidden, slope, shift, latents_near, w_in_near, w_out_near, seeds, bias, sems = refs
        members, points = latents.shape[:2]
        loads = [
            (latents.at[m, pl.ds(first, size), :], latents_near.at[m, pl.ds(first, size), :])
            for m in range(members)
        ]
        loads[1:1] = [(bias_in, bias), (w_out_ref, w_out_near)]
        loads[0:0] = [(w_in_ref, w_in_near), (seeds_in, seeds)]
        if size < points:
            rest = pl.ds(size, points - size)
            loads.append((latents.at[:, rest, :], latents_near.at[:, rest, :]))
        loads = [pltpu.make_async_copy(a, b, sems.at[k]) for k, (a, b) in enumerate(loads)]
        for load in loads[: 4 + members]:
            load.start()
        latents, w_in_ref, w_out_ref = latents_near, w_in_near, w_out_near
        loads[1].wait()
        loads[3].wait()
        for m in range(members):
            shift[m : m + 1, :] = bias[...] + noise_row(seeds[m], bias.shape[1])
        loads[0].wait()
        loads[4].wait()
        for load in loads[4 + members :]:
            load.start()
    else:
        _, shift, latents, w_in_ref, w_out_ref, outputs, hidden, slope = refs
    members = latents.shape[0]
    w_in = w_in_ref[...]
    w_out = w_out_ref[...]
    ahead = None
    behind = None

    def activate(k, rows, x):
        x2 = x * x
        half = 0.5 * jnp.tanh(x * (GELU_A + GELU_B * x2)) + 0.5
        h = x * half
        low = h.astype(BF16)
        hidden[k, rows, :] = low
        slope[k, rows, :] = half + (h - h * half) * (2.0 * GELU_A + 6.0 * GELU_B * x2)
        return k, rows, low

    def finish(k, rows, low):
        outputs[k, rows, :] = jnp.dot(low, w_out, preferred_element_type=F32).astype(BF16)

    for k in range(members):
        if stage:
            loads[2 if k == 0 else 4 + k].wait()
        for r in range(size // sub):
            rows = pl.ds(r * sub, sub)
            x = jnp.dot(latents[k, pl.ds(first + r * sub, sub), :], w_in, preferred_element_type=F32) + shift[k : k + 1, :]
            if behind is not None:
                finish(*behind)
            behind = activate(*ahead) if ahead is not None else None
            ahead = (k, rows, x)
    if behind is not None:
        finish(*behind)
    finish(*activate(*ahead))
    if stage:
        for load in loads[4 + members :]:
            load.wait()


def forward(arrays, first, size, after=None, sub=256):
    stage = after is None
    latents, weight_in, weight_out = arrays[-3:]
    members, _, depth = latents.shape
    width, variables = weight_out.shape
    near = pl.BlockSpec(memory_space=pltpu.VMEM)
    far = pl.BlockSpec(memory_space=pltpu.HBM)
    anywhere = pl.BlockSpec(memory_space=pl.ANY)
    shapes = [
        jax.ShapeDtypeStruct((members, size, variables), BF16),
        jax.ShapeDtypeStruct((members, size, width), BF16),
        jax.ShapeDtypeStruct((members, size, width), F32),
    ]
    scratch = []
    if stage:
        arrays = [in_hbm(v) for v in arrays]
        shapes.append(jax.ShapeDtypeStruct((members, width), F32))
        shapes += [jax.ShapeDtypeStruct(v.shape, v.dtype) for v in (latents, weight_in, weight_out)]
        scratch = [
            pltpu.SMEM((members,), jnp.int32),
            pltpu.VMEM((1, width), F32),
            pltpu.SemaphoreType.DMA((members + 5,)),
        ]
    return pl.pallas_call(
        partial(forward_body, first, size, piece_of(size, sub), stage),
        in_specs=[far] * len(arrays) if stage else [anywhere] + [near] * len(arrays),
        out_specs=[near] * len(shapes),
        out_shape=shapes,
        scratch_shapes=scratch,
        compiler_params=pltpu.CompilerParams(vmem_limit_bytes=VMEM_LIMIT),
        cost_estimate=pl.CostEstimate(
            flops=int(COST_F * members * size * width * (depth + variables)),
            bytes_accessed=0,
            transcendentals=0,
        ),
        name="forward",
    )(*arrays if stage else (after, *arrays))


def pair_tiles(own, others, targets, area, grad, start, unroll, first, loss_coef):
    members = own.shape[0]
    variables = own.shape[2]
    count = members * (1 + len(others))
    mine = members * TILE
    spots = [pl.multiple_of(start + u * TILE, TILE) for u in range(unroll)]
    ones = jnp.ones((8, 2 * variables), BF16)
    i = lax.broadcasted_iota(jnp.int32, (mine, count * TILE), 0)
    j = lax.broadcasted_iota(jnp.int32, (mine, count * TILE), 1)
    pair = jnp.logical_and(jnp.bitwise_and(i ^ j, TILE - 1) == 0, i != j)
    fulls, dists, weights = [], [], []
    for row in spots:
        rows = pl.ds(row, TILE)
        low = own[:, rows, :].reshape(mine, variables)
        full = jnp.concatenate(
            [low] + [o[:, rows, :].reshape(mine, variables) for o in others], axis=0
        )
        wide = full.astype(F32)
        square = wide * wide
        square_high = square.astype(BF16)
        square_low = (square - square_high.astype(F32)).astype(BF16)
        norms = nt(ones, jnp.concatenate([square_high, square_low], axis=1))[0:1, :] + EPSILON
        own_norms = jnp.sum(square[:mine], axis=1, keepdims=True)
        fulls.append(full)
        dists.append(jnp.maximum((own_norms + norms) - nt(low + low, full), EPSILON))
    for dist in dists:
        weight = jnp.where(pair, lax.rsqrt(dist), 0.0)
        total = jnp.sum(weight, axis=1, keepdims=True)
        weight_high = weight.astype(BF16)
        weight_low = (weight - weight_high.astype(F32)).astype(BF16)
        weights.append((total, jnp.concatenate([weight_high, weight_low], axis=0)))
    boths = [
        jnp.dot(weight, full, preferred_element_type=F32)
        for (_, weight), full in zip(weights, fulls)
    ]
    for row, full, both, (total, _) in zip(spots, fulls, boths, weights):
        mine_wide = full[:mine].astype(F32)
        weighted = both[:mine] + both[mine:]
        place = pl.ds(first + row, TILE)
        target = jnp.concatenate([targets[place, :]] * members, axis=0)
        scale = jnp.concatenate([area[place, :]] * members, axis=0)
        to_target = mine_wide - target
        spread = lax.rsqrt(jnp.sum(to_target * to_target, axis=1, keepdims=True) + EPSILON)
        pair_term = mine_wide * total - weighted
        value = scale * (
            to_target * (spread * (loss_coef / count)) - pair_term * (loss_coef / (count * (count - 1)))
        )
        grad[:, pl.ds(row, TILE), :] = value.astype(BF16).reshape(members, TILE, variables)


def backward_body(n_others, n_after, first, loss_coef, has_total, unroll, sub, dests, *refs):
    own, *refs = refs
    others, refs = refs[:n_others], refs[n_others:]
    targets, area, hidden, slope, latents, weight_out, *refs = refs
    if has_total:
        in_prior, out_prior, bias_prior, *refs = refs
    refs = refs[n_after:]
    if dests:
        keep, send, *refs = refs
    else:
        in_total, out_total, bias_total, *refs = refs
    grad, low = refs
    members, size, variables = own.shape

    @pl.loop(0, size // TILE // unroll)
    def _(t):
        pair_tiles(own, others, targets, area, grad, t * (unroll * TILE), unroll, first, loss_coef)

    w_out = weight_out[...]
    width = w_out.shape[0]
    bias_sum = bias_prior[...] if has_total else jnp.zeros((TILE, width), F32)
    for m in range(members):
        for r in range(size // sub):
            rows = pl.ds(r * sub, sub)
            pre = nt(grad[m, rows, :], w_out) * slope[m, rows, :]
            bias_sum += jnp.sum(pre.reshape(sub // TILE, TILE, width), axis=0)
            low[m, rows, :] = pre.astype(BF16)
    flat = lambda ref: ref[...].reshape(members * size, ref.shape[2])
    out_sum = tn(flat(hidden), flat(grad))
    depth = latents.shape[2]
    near = latents[:, pl.ds(first, size), :].reshape(members * size, depth)
    in_sum = tn(near, flat(low))
    if has_total:
        out_sum += out_prior[...]
        in_sum += in_prior[...]
    if not dests:
        in_total[...] = in_sum
        out_total[...] = out_sum
        bias_total[...] = bias_sum
        return
    core = lax.axis_index("mem") & 1
    share = in_sum.shape[0] // dests
    lanes = out_sum.shape[1]
    groups = width // lanes
    for half in range(2):
        for place in range(dests // 2):
            dest = 2 * place + half
            rows = slice(dest * share, (dest + 1) * share)
            block = jnp.concatenate(
                [in_sum[rows, q * lanes : (q + 1) * lanes] for q in range(groups)]
                + [out_sum[rows, :]]
                + [bias_sum[:, dest * share // lanes * lanes : (dest * share // lanes + 1) * lanes]],
                axis=0,
            )

            @pl.when(core == half)
            def _():
                keep[place] = block

            @pl.when(core != half)
            def _():
                send[place] = block


def backward(own, others, targets, area, hidden, slope, latents, weight_out, prior, first, loss_coef, dests=0, after=None, unroll=10, sub=256):
    members, size, variables = own.shape
    depth = latents.shape[2]
    width = weight_out.shape[0]
    whole = pl.BlockSpec(memory_space=pltpu.VMEM)
    count = members * (1 + len(others))
    if dests:
        rows = depth // dests * (width // variables + 1) + TILE
        shapes = [jax.ShapeDtypeStruct((dests // 2, rows, variables), F32)] * 2
    else:
        shapes = [
            jax.ShapeDtypeStruct((depth, width), F32),
            jax.ShapeDtypeStruct((width, variables), F32),
            jax.ShapeDtypeStruct((TILE, width), F32),
        ]
    return pl.pallas_call(
        partial(backward_body, len(others), 0 if after is None else 1, first, loss_coef, prior is not None, piece_of(size, unroll * TILE) // TILE, piece_of(size, sub), dests),
        in_specs=[whole] * (3 + len(others))
        + [whole] * 4
        + ([whole] * 3 if prior is not None else [])
        + ([pl.BlockSpec(memory_space=pl.ANY)] if after is not None else []),
        out_specs=[whole] * len(shapes),
        out_shape=shapes,
        scratch_shapes=[
            pltpu.VMEM((members, size, variables), BF16),
            pltpu.VMEM((members, size, width), BF16),
        ],
        compiler_params=pltpu.CompilerParams(vmem_limit_bytes=VMEM_LIMIT),
        cost_estimate=pl.CostEstimate(
            flops=int(COST_B * members * size * (width * (depth + 2 * variables) + count * TILE * variables * 3)),
            bytes_accessed=0,
            transcendentals=0,
        ),
        name="backward",
    )(own, *others, targets, area, hidden, slope, latents, weight_out, *(prior or ()), *(() if after is None else (after,)))


OFFSETS = ((1, 0), (2, 1), (2, 0), (3, 1), (3, 0), (1, 1), (0, 1))


def spread_body(keep, arrived, mine, *parts):
    z, x = lax.axis_index("pts"), lax.axis_index("mem") >> 1
    here = z * 2 + x
    mine[...] = keep[here] + arrived[here]
    for part, (dz, dx) in zip(parts, OFFSETS):
        there = (z ^ dz) * 2 + (x ^ dx)
        part[...] = (keep[there] + arrived[there]).astype(part.dtype)


def spread_out(keep, arrived, dtype):
    _, rows, lanes = keep.shape
    whole = pl.BlockSpec(memory_space=pltpu.VMEM)
    return pl.pallas_call(
        spread_body,
        in_specs=[whole, whole],
        out_specs=[whole] * (1 + len(OFFSETS)),
        out_shape=[jax.ShapeDtypeStruct((rows, lanes), F32)]
        + [jax.ShapeDtypeStruct((rows, lanes), dtype)] * len(OFFSETS),
        compiler_params=pltpu.CompilerParams(vmem_limit_bytes=SMALL_LIMIT),
        name="spread_out",
    )(keep, arrived)


def finish_body(share, mine, *refs):
    parts, (in_share, out_share, bias_share) = refs[:-3], refs[-3:]
    total = mine[...]
    for part in parts:
        total += part[...].astype(F32)
    lanes = total.shape[1]
    groups = in_share.shape[1] // lanes
    for q in range(groups):
        in_share[:, q * lanes : (q + 1) * lanes] = total[q * share : (q + 1) * share]
    out_share[...] = total[groups * share : (groups + 1) * share]
    row = jnp.sum(total[(groups + 1) * share :], axis=0, keepdims=True)
    place = lax.axis_index("mem")
    picked = row[:, :share]
    for k in range(1, lanes // share):
        picked = jnp.where(place == k, row[:, k * share : (k + 1) * share], picked)
    bias_share[...] = picked


def finish(mine, parts, share, width):
    lanes = mine.shape[1]
    whole = pl.BlockSpec(memory_space=pltpu.VMEM)
    return pl.pallas_call(
        partial(finish_body, share),
        in_specs=[whole] * (1 + len(parts)),
        out_specs=[whole] * 3,
        out_shape=[
            jax.ShapeDtypeStruct((share, width), F32),
            jax.ShapeDtypeStruct((share, lanes), F32),
            jax.ShapeDtypeStruct((1, share), F32),
        ],
        compiler_params=pltpu.CompilerParams(vmem_limit_bytes=SMALL_LIMIT),
        name="finish",
    )(mine, *parts)


def tie_body(value, after, tied):
    pass


def tie(value, after):
    anywhere = pl.BlockSpec(memory_space=pl.ANY)
    return pl.pallas_call(
        tie_body,
        in_specs=[anywhere] * 2,
        out_specs=anywhere,
        out_shape=jax.ShapeDtypeStruct(value.shape, value.dtype),
        input_output_aliases={0: 0},
        compiler_params=pltpu.CompilerParams(vmem_limit_bytes=TINY_LIMIT),
        name="tie",
    )(value, after)


def area_of(lat_row, rows_total):
    return jnp.cos(jnp.pi * (lat_row.astype(F32) + 0.5) / rows_total - jnp.pi / 2)


def swap_members(block, bit):
    size = lax.axis_size("mem")
    return lax.ppermute(block, "mem", [(i, i ^ bit) for i in range(size)])


def swap_points(block, dz, dx):
    points, members = lax.axis_size("pts"), lax.axis_size("mem")
    pairs = [
        (z * members + m, (z ^ dz) * members + (m ^ (2 * dx)))
        for z in range(points)
        for m in range(members)
    ]
    return lax.ppermute(block, ("pts", "mem"), pairs)


CHUNKS = (288, 288, 224, 224)


def chunks_of(points):
    scale = points // sum(CHUNKS)
    first = 0
    for size in CHUNKS:
        yield first, size * scale
        first += size * scale


def local(latents, member_seeds, targets, lat_row, weight_in, bias_in, weight_out):
    points = latents.shape[1]
    depth = latents.shape[2]
    width, variables = weight_out.shape
    devices_pts, devices_mem = lax.axis_size("pts"), lax.axis_size("mem")
    dests = devices_pts * devices_mem
    loss_coef = LOSS_SCALE / math.sqrt(points * devices_pts)
    area = jnp.broadcast_to(area_of(lat_row, LAT_ROWS)[:, None], (points, variables))
    packed = dests == 16 and devices_mem == 4
    plan = list(chunks_of(points))
    bits = [1 << k for k in reversed(range(devices_mem.bit_length() - 1))]
    saved = []
    out = None
    arrays = [member_seeds, bias_in[None, :], latents, weight_in, weight_out]
    for first, size in plan:
        out, hidden, slope, *staged = forward(arrays, first, size, after=out)
        arrays = staged or arrays
        saved.append([[out, swap_members(out, bits[0])], hidden, slope])
    total = None
    sums = []
    for k, (first, size) in enumerate(plan):
        held, hidden, slope = saved[k]
        if k and LAGS[k - 1] < k:
            held[1] = tie(held[1], sums[k - 1 - LAGS[k - 1]])
        for bit in bits[1:]:
            held = held + [swap_members(v, bit) for v in held]
        last = first + size == points
        total = list(backward(
            held[0], held[1:], targets, area, hidden, slope, arrays[1], arrays[3], total,
            first, loss_coef, dests if last and packed else 0,
            after=saved[-1][0][0] if k == 0 else None,
        ))
        sums.append(total[-1])
    if not packed:
        scatter = lambda v: lax.psum_scatter(v, ("pts", "mem"), scatter_dimension=0, tiled=True)
        return scatter(total[0]), scatter(total[1]), scatter(jnp.sum(total[2], axis=0))
    keep, send = total
    arrived = swap_members(send, 1)
    mine, *parts = spread_out(keep, arrived, LINK)
    parts = [swap_points(part, dz, dx) for part, (dz, dx) in zip(parts, OFFSETS)]
    in_share, out_share, bias_share = finish(mine, parts, depth // dests, width)
    return in_share, out_share, bias_share.reshape(depth // dests)


def solution(mesh):
    return jax.shard_map(
        local,
        mesh=mesh,
        in_specs=(
            P("mem", ("groups", "pts"), None),
            P(("groups", "mem")),
            P(("groups", "pts"), None),
            P(("groups", "pts")),
            P(),
            P(),
            P(),
        ),
        out_specs=(
            P(("groups", "pts", "mem"), None),
            P(("groups", "pts", "mem"), None),
            P(("groups", "pts", "mem")),
        ),
        check_vma=False,
    )
```

```python
from functools import partial
import math

import jax
import jax.numpy as jnp
from jax import lax
from jax.experimental import pallas as pl
from jax.experimental.pallas import tpu as pltpu
from jax.sharding import PartitionSpec as P

LAT_ROWS = 640
LOSS_SCALE = 256
EPSILON = 0.0001
TILE = 16
F32 = jnp.float32
BF16 = jnp.bfloat16
VMEM_LIMIT = 16 * 1024 * 1024
SMALL_LIMIT = 8 * 1024 * 1024
TINY_LIMIT = 1024 * 1024
LINK = BF16
COST_F = 2
COST_B = 8
LAGS = (1, 1, 1)
GELU_A = math.sqrt(2.0 / math.pi)
GELU_B = GELU_A * 0.044715


def nt(a, b):
    return lax.dot_general(a, b, (((1,), (1,)), ((), ())), preferred_element_type=F32)


def tn(a, b):
    return lax.dot_general(a, b, (((0,), (0,)), ((), ())), preferred_element_type=F32)


def in_hbm(v):
    return pltpu.with_memory_space_constraint(v, pltpu.HBM)


def piece_of(size, most):
    return max(k for k in range(TILE, most + 1, TILE) if size % k == 0)


def noise_row(seed, width):
    channel = lax.broadcasted_iota(jnp.int32, (1, width), 1)
    mixed = seed * (37 * channel + 11) + 7 * channel
    quotient = (mixed.astype(F32) * (1.0 / 65521.0)).astype(jnp.int32)
    rest = mixed - quotient * 65521
    rest = jnp.where(rest < 0, rest + 65521, rest)
    rest = jnp.where(rest >= 65521, rest - 65521, rest)
    return (rest.astype(F32) / 65521.0 - 0.5) * 2.0


def forward_body(first, size, sub, stage, *refs):
    if stage:
        seeds_in, bias_in, latents, w_in_ref, w_out_ref, *refs = refs
        outputs, hidden, slope, shift, latents_near, w_in_near, w_out_near, seeds, bias, sems = refs
        members, points = latents.shape[:2]
        loads = [
            (latents.at[m, pl.ds(first, size), :], latents_near.at[m, pl.ds(first, size), :])
            for m in range(members)
        ]
        loads[1:1] = [(bias_in, bias), (w_out_ref, w_out_near)]
        loads[0:0] = [(w_in_ref, w_in_near), (seeds_in, seeds)]
        if size < points:
            rest = pl.ds(size, points - size)
            loads.append((latents.at[:, rest, :], latents_near.at[:, rest, :]))
        loads = [pltpu.make_async_copy(a, b, sems.at[k]) for k, (a, b) in enumerate(loads)]
        for load in loads[: 4 + members]:
            load.start()
        latents, w_in_ref, w_out_ref = latents_near, w_in_near, w_out_near
        loads[1].wait()
        loads[3].wait()
        for m in range(members):
            shift[m : m + 1, :] = bias[...] + noise_row(seeds[m], bias.shape[1])
        loads[0].wait()
        loads[4].wait()
        for load in loads[4 + members :]:
            load.start()
    else:
        _, shift, latents, w_in_ref, w_out_ref, outputs, hidden, slope = refs
    members = latents.shape[0]
    w_in = w_in_ref[...]
    w_out = w_out_ref[...]
    ahead = None
    behind = None

    def activate(k, rows, x):
        x2 = x * x
        half = 0.5 * jnp.tanh(x * (GELU_A + GELU_B * x2)) + 0.5
        h = x * half
        low = h.astype(BF16)
        hidden[k, rows, :] = low
        slope[k, rows, :] = half + (h - h * half) * (2.0 * GELU_A + 6.0 * GELU_B * x2)
        return k, rows, low

    def finish(k, rows, low):
        outputs[k, rows, :] = jnp.dot(low, w_out, preferred_element_type=F32).astype(BF16)

    for k in range(members):
        if stage:
            loads[2 if k == 0 else 4 + k].wait()
        for r in range(size // sub):
            rows = pl.ds(r * sub, sub)
            x = jnp.dot(latents[k, pl.ds(first + r * sub, sub), :], w_in, preferred_element_type=F32) + shift[k : k + 1, :]
            if behind is not None:
                finish(*behind)
            behind = activate(*ahead) if ahead is not None else None
            ahead = (k, rows, x)
    if behind is not None:
        finish(*behind)
    finish(*activate(*ahead))
    if stage:
        for load in loads[4 + members :]:
            load.wait()


def forward(arrays, first, size, after=None, sub=256):
    stage = after is None
    latents, weight_in, weight_out = arrays[-3:]
    members, _, depth = latents.shape
    width, variables = weight_out.shape
    near = pl.BlockSpec(memory_space=pltpu.VMEM)
    far = pl.BlockSpec(memory_space=pltpu.HBM)
    anywhere = pl.BlockSpec(memory_space=pl.ANY)
    shapes = [
        jax.ShapeDtypeStruct((members, size, variables), BF16),
        jax.ShapeDtypeStruct((members, size, width), BF16),
        jax.ShapeDtypeStruct((members, size, width), F32),
    ]
    scratch = []
    if stage:
        arrays = [in_hbm(v) for v in arrays]
        shapes.append(jax.ShapeDtypeStruct((members, width), F32))
        shapes += [jax.ShapeDtypeStruct(v.shape, v.dtype) for v in (latents, weight_in, weight_out)]
        scratch = [
            pltpu.SMEM((members,), jnp.int32),
            pltpu.VMEM((1, width), F32),
            pltpu.SemaphoreType.DMA((members + 5,)),
        ]
    return pl.pallas_call(
        partial(forward_body, first, size, piece_of(size, sub), stage),
        in_specs=[far] * len(arrays) if stage else [anywhere] + [near] * len(arrays),
        out_specs=[near] * len(shapes),
        out_shape=shapes,
        scratch_shapes=scratch,
        compiler_params=pltpu.CompilerParams(vmem_limit_bytes=VMEM_LIMIT),
        cost_estimate=pl.CostEstimate(
            flops=int(COST_F * members * size * width * (depth + variables)),
            bytes_accessed=0,
            transcendentals=0,
        ),
        name="forward",
    )(*arrays if stage else (after, *arrays))


def pair_tiles(own, others, targets, area, grad, start, unroll, first, loss_coef):
    members = own.shape[0]
    variables = own.shape[2]
    count = members * (1 + len(others))
    mine = members * TILE
    spots = [pl.multiple_of(start + u * TILE, TILE) for u in range(unroll)]
    ones = jnp.ones((8, 2 * variables), BF16)
    i = lax.broadcasted_iota(jnp.int32, (mine, count * TILE), 0)
    j = lax.broadcasted_iota(jnp.int32, (mine, count * TILE), 1)
    pair = jnp.logical_and(jnp.bitwise_and(i ^ j, TILE - 1) == 0, i != j)
    fulls, dists, weights = [], [], []
    for row in spots:
        rows = pl.ds(row, TILE)
        low = own[:, rows, :].reshape(mine, variables)
        full = jnp.concatenate(
            [low] + [o[:, rows, :].reshape(mine, variables) for o in others], axis=0
        )
        wide = full.astype(F32)
        square = wide * wide
        square_high = square.astype(BF16)
        square_low = (square - square_high.astype(F32)).astype(BF16)
        norms = nt(ones, jnp.concatenate([square_high, square_low], axis=1))[0:1, :] + EPSILON
        own_norms = jnp.sum(square[:mine], axis=1, keepdims=True)
        fulls.append(full)
        dists.append(jnp.maximum((own_norms + norms) - nt(low + low, full), EPSILON))
    for dist in dists:
        weight = jnp.where(pair, lax.rsqrt(dist), 0.0)
        total = jnp.sum(weight, axis=1, keepdims=True)
        weight_high = weight.astype(BF16)
        weight_low = (weight - weight_high.astype(F32)).astype(BF16)
        weights.append((total, jnp.concatenate([weight_high, weight_low], axis=0)))
    boths = [
        jnp.dot(weight, full, preferred_element_type=F32)
        for (_, weight), full in zip(weights, fulls)
    ]
    for row, full, both, (total, _) in zip(spots, fulls, boths, weights):
        mine_wide = full[:mine].astype(F32)
        weighted = both[:mine] + both[mine:]
        place = pl.ds(first + row, TILE)
        target = jnp.concatenate([targets[place, :]] * members, axis=0)
        scale = jnp.concatenate([area[place, :]] * members, axis=0)
        to_target = mine_wide - target
        spread = lax.rsqrt(jnp.sum(to_target * to_target, axis=1, keepdims=True) + EPSILON)
        pair_term = mine_wide * total - weighted
        value = scale * (
            to_target * (spread * (loss_coef / count)) - pair_term * (loss_coef / (count * (count - 1)))
        )
        grad[:, pl.ds(row, TILE), :] = value.astype(BF16).reshape(members, TILE, variables)


def backward_body(n_others, n_after, first, loss_coef, has_total, unroll, sub, dests, *refs):
    own, *refs = refs
    others, refs = refs[:n_others], refs[n_others:]
    targets, area, hidden, slope, latents, weight_out, *refs = refs
    if has_total:
        in_prior, out_prior, bias_prior, *refs = refs
    refs = refs[n_after:]
    if dests:
        keep, send, *refs = refs
    else:
        in_total, out_total, bias_total, *refs = refs
    grad, low = refs
    members, size, variables = own.shape

    @pl.loop(0, size // TILE // unroll)
    def _(t):
        pair_tiles(own, others, targets, area, grad, t * (unroll * TILE), unroll, first, loss_coef)

    w_out = weight_out[...]
    width = w_out.shape[0]
    bias_sum = bias_prior[...] if has_total else jnp.zeros((TILE, width), F32)
    for m in range(members):
        for r in range(size // sub):
            rows = pl.ds(r * sub, sub)
            pre = nt(grad[m, rows, :], w_out) * slope[m, rows, :]
            bias_sum += jnp.sum(pre.reshape(sub // TILE, TILE, width), axis=0)
            low[m, rows, :] = pre.astype(BF16)
    flat = lambda ref: ref[...].reshape(members * size, ref.shape[2])
    out_sum = tn(flat(hidden), flat(grad))
    depth = latents.shape[2]
    near = latents[:, pl.ds(first, size), :].reshape(members * size, depth)
    in_sum = tn(near, flat(low))
    if has_total:
        out_sum += out_prior[...]
        in_sum += in_prior[...]
    if not dests:
        in_total[...] = in_sum
        out_total[...] = out_sum
        bias_total[...] = bias_sum
        return
    core = lax.axis_index("mem") & 1
    share = in_sum.shape[0] // dests
    lanes = out_sum.shape[1]
    groups = width // lanes
    for half in range(2):
        for place in range(dests // 2):
            dest = 2 * place + half
            rows = slice(dest * share, (dest + 1) * share)
            block = jnp.concatenate(
                [in_sum[rows, q * lanes : (q + 1) * lanes] for q in range(groups)]
                + [out_sum[rows, :]]
                + [bias_sum[:, dest * share // lanes * lanes : (dest * share // lanes + 1) * lanes]],
                axis=0,
            )

            @pl.when(core == half)
            def _():
                keep[place] = block

            @pl.when(core != half)
            def _():
                send[place] = block


def backward(own, others, targets, area, hidden, slope, latents, weight_out, prior, first, loss_coef, dests=0, after=None, unroll=18, sub=256):
    members, size, variables = own.shape
    depth = latents.shape[2]
    width = weight_out.shape[0]
    whole = pl.BlockSpec(memory_space=pltpu.VMEM)
    count = members * (1 + len(others))
    if dests:
        rows = depth // dests * (width // variables + 1) + TILE
        shapes = [jax.ShapeDtypeStruct((dests // 2, rows, variables), F32)] * 2
    else:
        shapes = [
            jax.ShapeDtypeStruct((depth, width), F32),
            jax.ShapeDtypeStruct((width, variables), F32),
            jax.ShapeDtypeStruct((TILE, width), F32),
        ]
    return pl.pallas_call(
        partial(backward_body, len(others), 0 if after is None else 1, first, loss_coef, prior is not None, piece_of(size, unroll * TILE) // TILE, piece_of(size, sub), dests),
        in_specs=[whole] * (3 + len(others))
        + [whole] * 4
        + ([whole] * 3 if prior is not None else [])
        + ([pl.BlockSpec(memory_space=pl.ANY)] if after is not None else []),
        out_specs=[whole] * len(shapes),
        out_shape=shapes,
        scratch_shapes=[
            pltpu.VMEM((members, size, variables), BF16),
            pltpu.VMEM((members, size, width), BF16),
        ],
        compiler_params=pltpu.CompilerParams(vmem_limit_bytes=VMEM_LIMIT),
        cost_estimate=pl.CostEstimate(
            flops=int(COST_B * members * size * (width * (depth + 2 * variables) + count * TILE * variables * 3)),
            bytes_accessed=0,
            transcendentals=0,
        ),
        name="backward",
    )(own, *others, targets, area, hidden, slope, latents, weight_out, *(prior or ()), *(() if after is None else (after,)))


OFFSETS = ((1, 0), (2, 1), (2, 0), (3, 1), (3, 0), (1, 1), (0, 1))


def spread_body(keep, arrived, mine, *parts):
    z, x = lax.axis_index("pts"), lax.axis_index("mem") >> 1
    here = z * 2 + x
    mine[...] = keep[here] + arrived[here]
    for part, (dz, dx) in zip(parts, OFFSETS):
        there = (z ^ dz) * 2 + (x ^ dx)
        part[...] = (keep[there] + arrived[there]).astype(part.dtype)


def spread_out(keep, arrived, dtype):
    _, rows, lanes = keep.shape
    whole = pl.BlockSpec(memory_space=pltpu.VMEM)
    return pl.pallas_call(
        spread_body,
        in_specs=[whole, whole],
        out_specs=[whole] * (1 + len(OFFSETS)),
        out_shape=[jax.ShapeDtypeStruct((rows, lanes), F32)]
        + [jax.ShapeDtypeStruct((rows, lanes), dtype)] * len(OFFSETS),
        compiler_params=pltpu.CompilerParams(vmem_limit_bytes=SMALL_LIMIT),
        name="spread_out",
    )(keep, arrived)


def finish_body(share, mine, *refs):
    parts, (in_share, out_share, bias_share) = refs[:-3], refs[-3:]
    total = mine[...]
    for part in parts:
        total += part[...].astype(F32)
    lanes = total.shape[1]
    groups = in_share.shape[1] // lanes
    for q in range(groups):
        in_share[:, q * lanes : (q + 1) * lanes] = total[q * share : (q + 1) * share]
    out_share[...] = total[groups * share : (groups + 1) * share]
    row = jnp.sum(total[(groups + 1) * share :], axis=0, keepdims=True)
    place = lax.axis_index("mem")
    picked = row[:, :share]
    for k in range(1, lanes // share):
        picked = jnp.where(place == k, row[:, k * share : (k + 1) * share], picked)
    bias_share[...] = picked


def finish(mine, parts, share, width):
    lanes = mine.shape[1]
    whole = pl.BlockSpec(memory_space=pltpu.VMEM)
    return pl.pallas_call(
        partial(finish_body, share),
        in_specs=[whole] * (1 + len(parts)),
        out_specs=[whole] * 3,
        out_shape=[
            jax.ShapeDtypeStruct((share, width), F32),
            jax.ShapeDtypeStruct((share, lanes), F32),
            jax.ShapeDtypeStruct((1, share), F32),
        ],
        compiler_params=pltpu.CompilerParams(vmem_limit_bytes=SMALL_LIMIT),
        name="finish",
    )(mine, *parts)


def tie_body(value, after, tied):
    pass


def tie(value, after):
    anywhere = pl.BlockSpec(memory_space=pl.ANY)
    return pl.pallas_call(
        tie_body,
        in_specs=[anywhere] * 2,
        out_specs=anywhere,
        out_shape=jax.ShapeDtypeStruct(value.shape, value.dtype),
        input_output_aliases={0: 0},
        compiler_params=pltpu.CompilerParams(vmem_limit_bytes=TINY_LIMIT),
        name="tie",
    )(value, after)


def area_of(lat_row, rows_total):
    return jnp.cos(jnp.pi * (lat_row.astype(F32) + 0.5) / rows_total - jnp.pi / 2)


def swap_members(block, bit):
    size = lax.axis_size("mem")
    return lax.ppermute(block, "mem", [(i, i ^ bit) for i in range(size)])


def swap_points(block, dz, dx):
    points, members = lax.axis_size("pts"), lax.axis_size("mem")
    pairs = [
        (z * members + m, (z ^ dz) * members + (m ^ (2 * dx)))
        for z in range(points)
        for m in range(members)
    ]
    return lax.ppermute(block, ("pts", "mem"), pairs)


CHUNKS = (288, 288, 224, 224)


def chunks_of(points):
    scale = points // sum(CHUNKS)
    first = 0
    for size in CHUNKS:
        yield first, size * scale
        first += size * scale


def local(latents, member_seeds, targets, lat_row, weight_in, bias_in, weight_out):
    points = latents.shape[1]
    depth = latents.shape[2]
    width, variables = weight_out.shape
    devices_pts, devices_mem = lax.axis_size("pts"), lax.axis_size("mem")
    dests = devices_pts * devices_mem
    loss_coef = LOSS_SCALE / math.sqrt(points * devices_pts)
    area = jnp.broadcast_to(area_of(lat_row, LAT_ROWS)[:, None], (points, variables))
    packed = dests == 16 and devices_mem == 4
    plan = list(chunks_of(points))
    bits = [1 << k for k in reversed(range(devices_mem.bit_length() - 1))]
    saved = []
    out = None
    arrays = [member_seeds, bias_in[None, :], latents, weight_in, weight_out]
    for first, size in plan:
        out, hidden, slope, *staged = forward(arrays, first, size, after=out)
        arrays = staged or arrays
        saved.append([[out, swap_members(out, bits[0])], hidden, slope])
    total = None
    sums = []
    for k, (first, size) in enumerate(plan):
        held, hidden, slope = saved[k]
        if k and LAGS[k - 1] < k:
            held[1] = tie(held[1], sums[k - 1 - LAGS[k - 1]])
        for bit in bits[1:]:
            held = held + [swap_members(v, bit) for v in held]
        last = first + size == points
        total = list(backward(
            held[0], held[1:], targets, area, hidden, slope, arrays[1], arrays[3], total,
            first, loss_coef, dests if last and packed else 0,
            after=saved[-1][0][0] if k == 0 else None,
        ))
        sums.append(total[-1])
    if not packed:
        scatter = lambda v: lax.psum_scatter(v, ("pts", "mem"), scatter_dimension=0, tiled=True)
        return scatter(total[0]), scatter(total[1]), scatter(jnp.sum(total[2], axis=0))
    keep, send = total
    arrived = swap_members(send, 1)
    mine, *parts = spread_out(keep, arrived, LINK)
    parts = [swap_points(part, dz, dx) for part, (dz, dx) in zip(parts, OFFSETS)]
    in_share, out_share, bias_share = finish(mine, parts, depth // dests, width)
    return in_share, out_share, bias_share.reshape(depth // dests)


def solution(mesh):
    return jax.shard_map(
        local,
        mesh=mesh,
        in_specs=(
            P("mem", ("groups", "pts"), None),
            P(("groups", "mem")),
            P(("groups", "pts"), None),
            P(("groups", "pts")),
            P(),
            P(),
            P(),
        ),
        out_specs=(
            P(("groups", "pts", "mem"), None),
            P(("groups", "pts", "mem"), None),
            P(("groups", "pts", "mem")),
        ),
        check_vma=False,
    )
```

```python
from functools import partial
import math

import jax
import jax.numpy as jnp
from jax import lax
from jax.experimental import pallas as pl
from jax.experimental.pallas import tpu as pltpu
from jax.sharding import PartitionSpec as P

LAT_ROWS = 640
LOSS_SCALE = 256
EPSILON = 0.0001
TILE = 16
F32 = jnp.float32
BF16 = jnp.bfloat16
VMEM_LIMIT = 16 * 1024 * 1024
SMALL_LIMIT = 8 * 1024 * 1024
TINY_LIMIT = 1024 * 1024
LINK = BF16
COST_F = 2
COST_B = 8
LAGS = (1, 1, 1)
GELU_A = math.sqrt(2.0 / math.pi)
GELU_B = GELU_A * 0.044715


def nt(a, b):
    return lax.dot_general(a, b, (((1,), (1,)), ((), ())), preferred_element_type=F32)


def tn(a, b):
    return lax.dot_general(a, b, (((0,), (0,)), ((), ())), preferred_element_type=F32)


def in_hbm(v):
    return pltpu.with_memory_space_constraint(v, pltpu.HBM)


def piece_of(size, most):
    return max(k for k in range(TILE, most + 1, TILE) if size % k == 0)


def noise_row(seed, width):
    channel = lax.broadcasted_iota(jnp.int32, (1, width), 1)
    mixed = seed * (37 * channel + 11) + 7 * channel
    quotient = (mixed.astype(F32) * (1.0 / 65521.0)).astype(jnp.int32)
    rest = mixed - quotient * 65521
    rest = jnp.where(rest < 0, rest + 65521, rest)
    rest = jnp.where(rest >= 65521, rest - 65521, rest)
    return (rest.astype(F32) / 65521.0 - 0.5) * 2.0


def forward_body(first, size, sub, stage, *refs):
    if stage:
        seeds_in, bias_in, latents, w_in_ref, w_out_ref, *refs = refs
        outputs, hidden, slope, shift, latents_near, w_in_near, w_out_near, seeds, bias, sems = refs
        members, points = latents.shape[:2]
        loads = [
            (latents.at[m, pl.ds(first, size), :], latents_near.at[m, pl.ds(first, size), :])
            for m in range(members)
        ]
        loads[1:1] = [(bias_in, bias), (w_out_ref, w_out_near)]
        loads[0:0] = [(w_in_ref, w_in_near), (seeds_in, seeds)]
        if size < points:
            rest = pl.ds(size, points - size)
            loads.append((latents.at[:, rest, :], latents_near.at[:, rest, :]))
        loads = [pltpu.make_async_copy(a, b, sems.at[k]) for k, (a, b) in enumerate(loads)]
        for load in loads[: 4 + members]:
            load.start()
        latents, w_in_ref, w_out_ref = latents_near, w_in_near, w_out_near
        loads[1].wait()
        loads[3].wait()
        for m in range(members):
            shift[m : m + 1, :] = bias[...] + noise_row(seeds[m], bias.shape[1])
        loads[0].wait()
        loads[4].wait()
        for load in loads[4 + members :]:
            load.start()
    else:
        _, shift, latents, w_in_ref, w_out_ref, outputs, hidden, slope = refs
    members = latents.shape[0]
    w_in = w_in_ref[...]
    w_out = w_out_ref[...]
    ahead = None
    behind = None

    def activate(k, rows, x):
        x2 = x * x
        half = 0.5 * jnp.tanh(x * (GELU_A + GELU_B * x2)) + 0.5
        h = x * half
        low = h.astype(BF16)
        hidden[k, rows, :] = low
        slope[k, rows, :] = half + (h - h * half) * (2.0 * GELU_A + 6.0 * GELU_B * x2)
        return k, rows, low

    def finish(k, rows, low):
        outputs[k, rows, :] = jnp.dot(low, w_out, preferred_element_type=F32).astype(BF16)

    for k in range(members):
        if stage:
            loads[2 if k == 0 else 4 + k].wait()
        for r in range(size // sub):
            rows = pl.ds(r * sub, sub)
            x = jnp.dot(latents[k, pl.ds(first + r * sub, sub), :], w_in, preferred_element_type=F32) + shift[k : k + 1, :]
            if behind is not None:
                finish(*behind)
            behind = activate(*ahead) if ahead is not None else None
            ahead = (k, rows, x)
    if behind is not None:
        finish(*behind)
    finish(*activate(*ahead))
    if stage:
        for load in loads[4 + members :]:
            load.wait()


def forward(arrays, first, size, after=None, sub=256):
    stage = after is None
    latents, weight_in, weight_out = arrays[-3:]
    members, _, depth = latents.shape
    width, variables = weight_out.shape
    near = pl.BlockSpec(memory_space=pltpu.VMEM)
    far = pl.BlockSpec(memory_space=pltpu.HBM)
    anywhere = pl.BlockSpec(memory_space=pl.ANY)
    shapes = [
        jax.ShapeDtypeStruct((members, size, variables), BF16),
        jax.ShapeDtypeStruct((members, size, width), BF16),
        jax.ShapeDtypeStruct((members, size, width), F32),
    ]
    scratch = []
    if stage:
        arrays = [in_hbm(v) for v in arrays]
        shapes.append(jax.ShapeDtypeStruct((members, width), F32))
        shapes += [jax.ShapeDtypeStruct(v.shape, v.dtype) for v in (latents, weight_in, weight_out)]
        scratch = [
            pltpu.SMEM((members,), jnp.int32),
            pltpu.VMEM((1, width), F32),
            pltpu.SemaphoreType.DMA((members + 5,)),
        ]
    return pl.pallas_call(
        partial(forward_body, first, size, piece_of(size, sub), stage),
        in_specs=[far] * len(arrays) if stage else [anywhere] + [near] * len(arrays),
        out_specs=[near] * len(shapes),
        out_shape=shapes,
        scratch_shapes=scratch,
        compiler_params=pltpu.CompilerParams(vmem_limit_bytes=VMEM_LIMIT),
        cost_estimate=pl.CostEstimate(
            flops=int(COST_F * members * size * width * (depth + variables)),
            bytes_accessed=0,
            transcendentals=0,
        ),
        name="forward",
    )(*arrays if stage else (after, *arrays))


def pair_tiles(own, others, targets, area, grad, start, unroll, first, loss_coef):
    members = own.shape[0]
    variables = own.shape[2]
    count = members * (1 + len(others))
    mine = members * TILE
    spots = [pl.multiple_of(start + u * TILE, TILE) for u in range(unroll)]
    ones = jnp.ones((8, 2 * variables), BF16)
    i = lax.broadcasted_iota(jnp.int32, (mine, count * TILE), 0)
    j = lax.broadcasted_iota(jnp.int32, (mine, count * TILE), 1)
    pair = jnp.logical_and(jnp.bitwise_and(i ^ j, TILE - 1) == 0, i != j)
    fulls, dists, weights = [], [], []
    for row in spots:
        rows = pl.ds(row, TILE)
        low = own[:, rows, :].reshape(mine, variables)
        full = jnp.concatenate(
            [low] + [o[:, rows, :].reshape(mine, variables) for o in others], axis=0
        )
        wide = full.astype(F32)
        square = wide * wide
        square_high = square.astype(BF16)
        square_low = (square - square_high.astype(F32)).astype(BF16)
        norms = nt(ones, jnp.concatenate([square_high, square_low], axis=1))[0:1, :] + EPSILON
        own_norms = jnp.sum(square[:mine], axis=1, keepdims=True)
        fulls.append(full)
        dists.append(jnp.maximum((own_norms + norms) - nt(low + low, full), EPSILON))
    for dist in dists:
        weight = jnp.where(pair, lax.rsqrt(dist), 0.0)
        total = jnp.sum(weight, axis=1, keepdims=True)
        weight_high = weight.astype(BF16)
        weight_low = (weight - weight_high.astype(F32)).astype(BF16)
        weights.append((total, jnp.concatenate([weight_high, weight_low], axis=0)))
    boths = [
        jnp.dot(weight, full, preferred_element_type=F32)
        for (_, weight), full in zip(weights, fulls)
    ]
    for row, full, both, (total, _) in zip(spots, fulls, boths, weights):
        mine_wide = full[:mine].astype(F32)
        weighted = both[:mine] + both[mine:]
        place = pl.ds(first + row, TILE)
        target = jnp.concatenate([targets[place, :]] * members, axis=0)
        scale = jnp.concatenate([area[place, :]] * members, axis=0)
        to_target = mine_wide - target
        spread = lax.rsqrt(jnp.sum(to_target * to_target, axis=1, keepdims=True) + EPSILON)
        pair_term = mine_wide * total - weighted
        value = scale * (
            to_target * (spread * (loss_coef / count)) - pair_term * (loss_coef / (count * (count - 1)))
        )
        grad[:, pl.ds(row, TILE), :] = value.astype(BF16).reshape(members, TILE, variables)


def backward_body(n_others, n_after, first, loss_coef, has_total, unroll, sub, dests, *refs):
    own, *refs = refs
    others, refs = refs[:n_others], refs[n_others:]
    targets, area, hidden, slope, latents, weight_out, *refs = refs
    if has_total:
        in_prior, out_prior, bias_prior, *refs = refs
    refs = refs[n_after:]
    if dests:
        keep, send, *refs = refs
    else:
        in_total, out_total, bias_total, *refs = refs
    grad, low = refs
    members, size, variables = own.shape

    @pl.loop(0, size // TILE // unroll)
    def _(t):
        pair_tiles(own, others, targets, area, grad, t * (unroll * TILE), unroll, first, loss_coef)

    w_out = weight_out[...]
    width = w_out.shape[0]
    bias_sum = bias_prior[...] if has_total else jnp.zeros((TILE, width), F32)
    for m in range(members):
        for r in range(size // sub):
            rows = pl.ds(r * sub, sub)
            pre = nt(grad[m, rows, :], w_out) * slope[m, rows, :]
            bias_sum += jnp.sum(pre.reshape(sub // TILE, TILE, width), axis=0)
            low[m, rows, :] = pre.astype(BF16)
    flat = lambda ref: ref[...].reshape(members * size, ref.shape[2])
    out_sum = tn(flat(hidden), flat(grad))
    depth = latents.shape[2]
    near = latents[:, pl.ds(first, size), :].reshape(members * size, depth)
    in_sum = tn(near, flat(low))
    if has_total:
        out_sum += out_prior[...]
        in_sum += in_prior[...]
    if not dests:
        in_total[...] = in_sum
        out_total[...] = out_sum
        bias_total[...] = bias_sum
        return
    core = lax.axis_index("mem") & 1
    share = in_sum.shape[0] // dests
    lanes = out_sum.shape[1]
    groups = width // lanes
    for half in range(2):
        for place in range(dests // 2):
            dest = 2 * place + half
            rows = slice(dest * share, (dest + 1) * share)
            block = jnp.concatenate(
                [in_sum[rows, q * lanes : (q + 1) * lanes] for q in range(groups)]
                + [out_sum[rows, :]]
                + [bias_sum[:, dest * share // lanes * lanes : (dest * share // lanes + 1) * lanes]],
                axis=0,
            )

            @pl.when(core == half)
            def _():
                keep[place] = block

            @pl.when(core != half)
            def _():
                send[place] = block.astype(send.dtype)


def backward(own, others, targets, area, hidden, slope, latents, weight_out, prior, first, loss_coef, dests=0, send_dtype=F32, after=None, unroll=18, sub=256):
    members, size, variables = own.shape
    depth = latents.shape[2]
    width = weight_out.shape[0]
    whole = pl.BlockSpec(memory_space=pltpu.VMEM)
    count = members * (1 + len(others))
    if dests:
        rows = depth // dests * (width // variables + 1) + TILE
        shapes = [
            jax.ShapeDtypeStruct((dests // 2, rows, variables), dtype) for dtype in (F32, send_dtype)
        ]
    else:
        shapes = [
            jax.ShapeDtypeStruct((depth, width), F32),
            jax.ShapeDtypeStruct((width, variables), F32),
            jax.ShapeDtypeStruct((TILE, width), F32),
        ]
    return pl.pallas_call(
        partial(backward_body, len(others), 0 if after is None else 1, first, loss_coef, prior is not None, piece_of(size, unroll * TILE) // TILE, piece_of(size, sub), dests),
        in_specs=[whole] * (3 + len(others))
        + [whole] * 4
        + ([whole] * 3 if prior is not None else [])
        + ([pl.BlockSpec(memory_space=pl.ANY)] if after is not None else []),
        out_specs=[whole] * len(shapes),
        out_shape=shapes,
        scratch_shapes=[
            pltpu.VMEM((members, size, variables), BF16),
            pltpu.VMEM((members, size, width), BF16),
        ],
        compiler_params=pltpu.CompilerParams(vmem_limit_bytes=VMEM_LIMIT),
        cost_estimate=pl.CostEstimate(
            flops=int(COST_B * members * size * (width * (depth + 2 * variables) + count * TILE * variables * 3)),
            bytes_accessed=0,
            transcendentals=0,
        ),
        name="backward",
    )(own, *others, targets, area, hidden, slope, latents, weight_out, *(prior or ()), *(() if after is None else (after,)))


OFFSETS = ((1, 0), (2, 1), (2, 0), (3, 1), (3, 0), (1, 1), (0, 1))


def spread_body(n_sums, *refs):
    sums, (mine, *parts) = refs[:n_sums], refs[n_sums:]
    z, x = lax.axis_index("pts"), lax.axis_index("mem") >> 1
    here = z * 2 + x
    total = lambda place: sum(ref[place].astype(F32) for ref in sums)
    mine[...] = total(here)
    for part, (dz, dx) in zip(parts, OFFSETS):
        there = (z ^ dz) * 2 + (x ^ dx)
        part[...] = total(there).astype(part.dtype)


def spread_out(sums, dtype):
    _, rows, lanes = sums[0].shape
    whole = pl.BlockSpec(memory_space=pltpu.VMEM)
    return pl.pallas_call(
        partial(spread_body, len(sums)),
        in_specs=[whole] * len(sums),
        out_specs=[whole] * (1 + len(OFFSETS)),
        out_shape=[jax.ShapeDtypeStruct((rows, lanes), F32)]
        + [jax.ShapeDtypeStruct((rows, lanes), dtype)] * len(OFFSETS),
        compiler_params=pltpu.CompilerParams(vmem_limit_bytes=SMALL_LIMIT),
        name="spread_out",
    )(*sums)


def finish_body(share, mine, *refs):
    parts, (in_share, out_share, bias_share) = refs[:-3], refs[-3:]
    total = mine[...]
    for part in parts:
        total += part[...].astype(F32)
    lanes = total.shape[1]
    groups = in_share.shape[1] // lanes
    for q in range(groups):
        in_share[:, q * lanes : (q + 1) * lanes] = total[q * share : (q + 1) * share]
    out_share[...] = total[groups * share : (groups + 1) * share]
    row = jnp.sum(total[(groups + 1) * share :], axis=0, keepdims=True)
    place = lax.axis_index("mem")
    picked = row[:, :share]
    for k in range(1, lanes // share):
        picked = jnp.where(place == k, row[:, k * share : (k + 1) * share], picked)
    bias_share[...] = picked


def finish(mine, parts, share, width):
    lanes = mine.shape[1]
    whole = pl.BlockSpec(memory_space=pltpu.VMEM)
    return pl.pallas_call(
        partial(finish_body, share),
        in_specs=[whole] * (1 + len(parts)),
        out_specs=[whole] * 3,
        out_shape=[
            jax.ShapeDtypeStruct((share, width), F32),
            jax.ShapeDtypeStruct((share, lanes), F32),
            jax.ShapeDtypeStruct((1, share), F32),
        ],
        compiler_params=pltpu.CompilerParams(vmem_limit_bytes=SMALL_LIMIT),
        name="finish",
    )(mine, *parts)


def tie_body(value, after, tied):
    pass


def tie(value, after):
    anywhere = pl.BlockSpec(memory_space=pl.ANY)
    return pl.pallas_call(
        tie_body,
        in_specs=[anywhere] * 2,
        out_specs=anywhere,
        out_shape=jax.ShapeDtypeStruct(value.shape, value.dtype),
        input_output_aliases={0: 0},
        compiler_params=pltpu.CompilerParams(vmem_limit_bytes=TINY_LIMIT),
        name="tie",
    )(value, after)


def area_of(lat_row, rows_total):
    return jnp.cos(jnp.pi * (lat_row.astype(F32) + 0.5) / rows_total - jnp.pi / 2)


def swap_members(block, bit):
    size = lax.axis_size("mem")
    return lax.ppermute(block, "mem", [(i, i ^ bit) for i in range(size)])


def swap_points(block, dz, dx):
    points, members = lax.axis_size("pts"), lax.axis_size("mem")
    pairs = [
        (z * members + m, (z ^ dz) * members + (m ^ (2 * dx)))
        for z in range(points)
        for m in range(members)
    ]
    return lax.ppermute(block, ("pts", "mem"), pairs)


CHUNKS = (288, 288, 224, 224)


def chunks_of(points):
    scale = points // sum(CHUNKS)
    first = 0
    for size in CHUNKS:
        yield first, size * scale
        first += size * scale


def local(latents, member_seeds, targets, lat_row, weight_in, bias_in, weight_out):
    points = latents.shape[1]
    depth = latents.shape[2]
    width, variables = weight_out.shape
    devices_pts, devices_mem = lax.axis_size("pts"), lax.axis_size("mem")
    dests = devices_pts * devices_mem
    loss_coef = LOSS_SCALE / math.sqrt(points * devices_pts)
    area = jnp.broadcast_to(area_of(lat_row, LAT_ROWS)[:, None], (points, variables))
    packed = dests == 16 and devices_mem == 4
    plan = list(chunks_of(points))
    bits = [1 << k for k in reversed(range(devices_mem.bit_length() - 1))]
    saved = []
    out = None
    arrays = [member_seeds, bias_in[None, :], latents, weight_in, weight_out]
    for first, size in plan:
        out, hidden, slope, *staged = forward(arrays, first, size, after=out)
        arrays = staged or arrays
        saved.append([[out, swap_members(out, bits[0])], hidden, slope])
    total = None
    sums = []
    for k, (first, size) in enumerate(plan):
        held, hidden, slope = saved[k]
        if k and LAGS[k - 1] < k:
            held[1] = tie(held[1], sums[k - 1 - LAGS[k - 1]])
        for bit in bits[1:]:
            held = held + [swap_members(v, bit) for v in held]
        last = first + size == points
        split = packed and last and k > 0
        if split:
            early = total[0], swap_members(total[1], 1)
        after = saved[-1][0][0] if k == 0 else total[0] if split else None
        total = list(backward(
            held[0], held[1:], targets, area, hidden, slope, arrays[1], arrays[3],
            None if split else total, first, loss_coef,
            dests if packed and k >= len(plan) - 2 else 0,
            LINK if last else F32, after=after,
        ))
        sums.append(total[-1])
    if not packed:
        scatter = lambda v: lax.psum_scatter(v, ("pts", "mem"), scatter_dimension=0, tiled=True)
        return scatter(total[0]), scatter(total[1]), scatter(jnp.sum(total[2], axis=0))
    keep, send = total
    arrived = swap_members(send, 1)
    mine, *parts = spread_out([*early, keep, arrived], LINK)
    parts = [swap_points(part, dz, dx) for part, (dz, dx) in zip(parts, OFFSETS)]
    in_share, out_share, bias_share = finish(mine, parts, depth // dests, width)
    return in_share, out_share, bias_share.reshape(depth // dests)


def solution(mesh):
    return jax.shard_map(
        local,
        mesh=mesh,
        in_specs=(
            P("mem", ("groups", "pts"), None),
            P(("groups", "mem")),
            P(("groups", "pts"), None),
            P(("groups", "pts")),
            P(),
            P(),
            P(),
        ),
        out_specs=(
            P(("groups", "pts", "mem"), None),
            P(("groups", "pts", "mem"), None),
            P(("groups", "pts", "mem")),
        ),
        check_vma=False,
    )
```

```python
from functools import partial
import math

import jax
import jax.numpy as jnp
from jax import lax
from jax.experimental import pallas as pl
from jax.experimental.pallas import tpu as pltpu
from jax.sharding import PartitionSpec as P

LAT_ROWS = 640
LOSS_SCALE = 256
EPSILON = 0.0001
TILE = 16
F32 = jnp.float32
BF16 = jnp.bfloat16
VMEM_LIMIT = 16 * 1024 * 1024
SMALL_LIMIT = 8 * 1024 * 1024
TINY_LIMIT = 1024 * 1024
LINK = BF16
COST_F = 2
COST_B = 8
LAGS = (1, 1, 1)
GELU_A = math.sqrt(2.0 / math.pi)
GELU_B = GELU_A * 0.044715


def nt(a, b):
    return lax.dot_general(a, b, (((1,), (1,)), ((), ())), preferred_element_type=F32)


def tn(a, b):
    return lax.dot_general(a, b, (((0,), (0,)), ((), ())), preferred_element_type=F32)


def in_hbm(v):
    return pltpu.with_memory_space_constraint(v, pltpu.HBM)


def piece_of(size, most):
    return max(k for k in range(TILE, most + 1, TILE) if size % k == 0)


def noise_row(seed, width):
    channel = lax.broadcasted_iota(jnp.int32, (1, width), 1)
    mixed = seed * (37 * channel + 11) + 7 * channel
    quotient = (mixed.astype(F32) * (1.0 / 65521.0)).astype(jnp.int32)
    rest = mixed - quotient * 65521
    rest = jnp.where(rest < 0, rest + 65521, rest)
    rest = jnp.where(rest >= 65521, rest - 65521, rest)
    return (rest.astype(F32) / 65521.0 - 0.5) * 2.0


def forward_body(first, size, sub, stage, *refs):
    if stage:
        seeds_in, bias_in, latents, w_in_ref, w_out_ref, *refs = refs
        outputs, hidden, slope, shift, latents_near, w_in_near, w_out_near, seeds, bias, sems = refs
        members, points = latents.shape[:2]
        loads = [
            (latents.at[m, pl.ds(first, size), :], latents_near.at[m, pl.ds(first, size), :])
            for m in range(members)
        ]
        loads[1:1] = [(bias_in, bias), (w_out_ref, w_out_near)]
        loads[0:0] = [(w_in_ref, w_in_near), (seeds_in, seeds)]
        if size < points:
            rest = pl.ds(size, points - size)
            loads.append((latents.at[:, rest, :], latents_near.at[:, rest, :]))
        loads = [pltpu.make_async_copy(a, b, sems.at[k]) for k, (a, b) in enumerate(loads)]
        for load in loads[: 4 + members]:
            load.start()
        latents, w_in_ref, w_out_ref = latents_near, w_in_near, w_out_near
        loads[1].wait()
        loads[3].wait()
        for m in range(members):
            shift[m : m + 1, :] = bias[...] + noise_row(seeds[m], bias.shape[1])
        loads[0].wait()
        loads[4].wait()
        for load in loads[4 + members :]:
            load.start()
    else:
        _, shift, latents, w_in_ref, w_out_ref, outputs, hidden, slope = refs
    members = latents.shape[0]
    w_in = w_in_ref[...]
    w_out = w_out_ref[...]
    ahead = None
    behind = None

    def activate(k, rows, x):
        x2 = x * x
        half = 0.5 * jnp.tanh(x * (GELU_A + GELU_B * x2)) + 0.5
        h = x * half
        low = h.astype(BF16)
        hidden[k, rows, :] = low
        slope[k, rows, :] = half + (h - h * half) * (2.0 * GELU_A + 6.0 * GELU_B * x2)
        return k, rows, low

    def finish(k, rows, low):
        outputs[k, rows, :] = jnp.dot(low, w_out, preferred_element_type=F32).astype(BF16)

    for k in range(members):
        if stage:
            loads[2 if k == 0 else 4 + k].wait()
        for r in range(size // sub):
            rows = pl.ds(r * sub, sub)
            x = jnp.dot(latents[k, pl.ds(first + r * sub, sub), :], w_in, preferred_element_type=F32) + shift[k : k + 1, :]
            if behind is not None:
                finish(*behind)
            behind = activate(*ahead) if ahead is not None else None
            ahead = (k, rows, x)
    if behind is not None:
        finish(*behind)
    finish(*activate(*ahead))
    if stage:
        for load in loads[4 + members :]:
            load.wait()


def forward(arrays, first, size, after=None, sub=256):
    stage = after is None
    latents, weight_in, weight_out = arrays[-3:]
    members, _, depth = latents.shape
    width, variables = weight_out.shape
    near = pl.BlockSpec(memory_space=pltpu.VMEM)
    far = pl.BlockSpec(memory_space=pltpu.HBM)
    anywhere = pl.BlockSpec(memory_space=pl.ANY)
    shapes = [
        jax.ShapeDtypeStruct((members, size, variables), BF16),
        jax.ShapeDtypeStruct((members, size, width), BF16),
        jax.ShapeDtypeStruct((members, size, width), F32),
    ]
    scratch = []
    if stage:
        arrays = [in_hbm(v) for v in arrays]
        shapes.append(jax.ShapeDtypeStruct((members, width), F32))
        shapes += [jax.ShapeDtypeStruct(v.shape, v.dtype) for v in (latents, weight_in, weight_out)]
        scratch = [
            pltpu.SMEM((members,), jnp.int32),
            pltpu.VMEM((1, width), F32),
            pltpu.SemaphoreType.DMA((members + 5,)),
        ]
    return pl.pallas_call(
        partial(forward_body, first, size, piece_of(size, sub), stage),
        in_specs=[far] * len(arrays) if stage else [anywhere] + [near] * len(arrays),
        out_specs=[near] * len(shapes),
        out_shape=shapes,
        scratch_shapes=scratch,
        compiler_params=pltpu.CompilerParams(vmem_limit_bytes=VMEM_LIMIT),
        cost_estimate=pl.CostEstimate(
            flops=int(COST_F * members * size * width * (depth + variables)),
            bytes_accessed=0,
            transcendentals=0,
        ),
        name="forward",
    )(*arrays if stage else (after, *arrays))


def pair_tiles(own, others, targets, area, grad, start, unroll, first, loss_coef):
    members = own.shape[0]
    variables = own.shape[2]
    count = members * (1 + len(others))
    mine = members * TILE
    spots = [pl.multiple_of(start + u * TILE, TILE) for u in range(unroll)]
    ones = jnp.ones((8, 2 * variables), BF16)
    i = lax.broadcasted_iota(jnp.int32, (mine, count * TILE), 0)
    j = lax.broadcasted_iota(jnp.int32, (mine, count * TILE), 1)
    pair = jnp.logical_and(jnp.bitwise_and(i ^ j, TILE - 1) == 0, i != j)
    fulls, dists, weights = [], [], []
    for row in spots:
        rows = pl.ds(row, TILE)
        low = own[:, rows, :].reshape(mine, variables)
        full = jnp.concatenate(
            [low] + [o[:, rows, :].reshape(mine, variables) for o in others], axis=0
        )
        wide = full.astype(F32)
        square = wide * wide
        square_high = square.astype(BF16)
        square_low = (square - square_high.astype(F32)).astype(BF16)
        norms = nt(ones, jnp.concatenate([square_high, square_low], axis=1))[0:1, :] + EPSILON
        own_norms = jnp.sum(square[:mine], axis=1, keepdims=True)
        fulls.append(full)
        dists.append(jnp.maximum((own_norms + norms) - nt(low + low, full), EPSILON))
    for dist in dists:
        weight = jnp.where(pair, lax.rsqrt(dist), 0.0)
        total = jnp.sum(weight, axis=1, keepdims=True)
        weight_high = weight.astype(BF16)
        weight_low = (weight - weight_high.astype(F32)).astype(BF16)
        weights.append((total, jnp.concatenate([weight_high, weight_low], axis=0)))
    boths = [
        jnp.dot(weight, full, preferred_element_type=F32)
        for (_, weight), full in zip(weights, fulls)
    ]
    for row, full, both, (total, _) in zip(spots, fulls, boths, weights):
        mine_wide = full[:mine].astype(F32)
        weighted = both[:mine] + both[mine:]
        place = pl.ds(first + row, TILE)
        target = jnp.concatenate([targets[place, :]] * members, axis=0)
        scale = jnp.concatenate([area[place, :]] * members, axis=0)
        to_target = mine_wide - target
        spread = lax.rsqrt(jnp.sum(to_target * to_target, axis=1, keepdims=True) + EPSILON)
        pair_term = mine_wide * total - weighted
        value = scale * (
            to_target * (spread * (loss_coef / count)) - pair_term * (loss_coef / (count * (count - 1)))
        )
        grad[:, pl.ds(row, TILE), :] = value.astype(BF16).reshape(members, TILE, variables)


def backward_body(n_others, n_after, first, loss_coef, has_total, unroll, sub, dests, *refs):
    own, *refs = refs
    others, refs = refs[:n_others], refs[n_others:]
    targets, area, hidden, slope, latents, weight_out, *refs = refs
    if has_total:
        in_prior, out_prior, bias_prior, *refs = refs
    refs = refs[n_after:]
    if dests:
        keep, send, *refs = refs
    else:
        in_total, out_total, bias_total, *refs = refs
    grad, low = refs
    members, size, variables = own.shape

    @pl.loop(0, size // TILE // unroll)
    def _(t):
        pair_tiles(own, others, targets, area, grad, t * (unroll * TILE), unroll, first, loss_coef)

    w_out = weight_out[...]
    width = w_out.shape[0]
    bias_sum = bias_prior[...] if has_total else jnp.zeros((TILE, width), F32)
    for m in range(members):
        for r in range(size // sub):
            rows = pl.ds(r * sub, sub)
            pre = nt(grad[m, rows, :], w_out) * slope[m, rows, :]
            bias_sum += jnp.sum(pre.reshape(sub // TILE, TILE, width), axis=0)
            low[m, rows, :] = pre.astype(BF16)
    flat = lambda ref: ref[...].reshape(members * size, ref.shape[2])
    out_sum = tn(flat(hidden), flat(grad))
    depth = latents.shape[2]
    near = latents[:, pl.ds(first, size), :].reshape(members * size, depth)
    in_sum = tn(near, flat(low))
    if has_total:
        out_sum += out_prior[...]
        in_sum += in_prior[...]
    if not dests:
        in_total[...] = in_sum
        out_total[...] = out_sum
        bias_total[...] = bias_sum
        return
    core = lax.axis_index("mem") & 1
    share = in_sum.shape[0] // dests
    lanes = out_sum.shape[1]
    groups = width // lanes
    for half in range(2):
        for place in range(dests // 2):
            dest = 2 * place + half
            rows = slice(dest * share, (dest + 1) * share)
            block = jnp.concatenate(
                [in_sum[rows, q * lanes : (q + 1) * lanes] for q in range(groups)]
                + [out_sum[rows, :]]
                + [bias_sum[:, dest * share // lanes * lanes : (dest * share // lanes + 1) * lanes]],
                axis=0,
            )

            @pl.when(core == half)
            def _():
                keep[place] = block

            @pl.when(core != half)
            def _():
                send[place] = block


def backward(own, others, targets, area, hidden, slope, latents, weight_out, prior, first, loss_coef, dests=0, after=None, unroll=18, sub=256):
    members, size, variables = own.shape
    depth = latents.shape[2]
    width = weight_out.shape[0]
    whole = pl.BlockSpec(memory_space=pltpu.VMEM)
    count = members * (1 + len(others))
    if dests:
        rows = depth // dests * (width // variables + 1) + TILE
        shapes = [jax.ShapeDtypeStruct((dests // 2, rows, variables), F32)] * 2
    else:
        shapes = [
            jax.ShapeDtypeStruct((depth, width), F32),
            jax.ShapeDtypeStruct((width, variables), F32),
            jax.ShapeDtypeStruct((TILE, width), F32),
        ]
    return pl.pallas_call(
        partial(backward_body, len(others), 0 if after is None else 1, first, loss_coef, prior is not None, piece_of(size, unroll * TILE) // TILE, piece_of(size, sub), dests),
        in_specs=[whole] * (3 + len(others))
        + [whole] * 4
        + ([whole] * 3 if prior is not None else [])
        + ([pl.BlockSpec(memory_space=pl.ANY)] if after is not None else []),
        out_specs=[whole] * len(shapes),
        out_shape=shapes,
        scratch_shapes=[
            pltpu.VMEM((members, size, variables), BF16),
            pltpu.VMEM((members, size, width), BF16),
        ],
        compiler_params=pltpu.CompilerParams(vmem_limit_bytes=VMEM_LIMIT),
        cost_estimate=pl.CostEstimate(
            flops=int(COST_B * members * size * (width * (depth + 2 * variables) + count * TILE * variables * 3)),
            bytes_accessed=0,
            transcendentals=0,
        ),
        name="backward",
    )(own, *others, targets, area, hidden, slope, latents, weight_out, *(prior or ()), *(() if after is None else (after,)))


OFFSETS = ((1, 0), (2, 1), (2, 0), (3, 1), (3, 0), (1, 1), (0, 1))


def spread_body(keep, arrived, mine, *parts):
    z, x = lax.axis_index("pts"), lax.axis_index("mem") >> 1
    here = z * 2 + x
    mine[...] = keep[here] + arrived[here]
    for part, (dz, dx) in zip(parts, OFFSETS):
        there = (z ^ dz) * 2 + (x ^ dx)
        part[...] = (keep[there] + arrived[there]).astype(part.dtype)


def spread_out(keep, arrived, dtype):
    _, rows, lanes = keep.shape
    whole = pl.BlockSpec(memory_space=pltpu.VMEM)
    return pl.pallas_call(
        spread_body,
        in_specs=[whole, whole],
        out_specs=[whole] * (1 + len(OFFSETS)),
        out_shape=[jax.ShapeDtypeStruct((rows, lanes), F32)]
        + [jax.ShapeDtypeStruct((rows, lanes), dtype)] * len(OFFSETS),
        compiler_params=pltpu.CompilerParams(vmem_limit_bytes=SMALL_LIMIT),
        name="spread_out",
    )(keep, arrived)


def finish_body(share, mine, *refs):
    parts, (in_share, out_share, bias_share) = refs[:-3], refs[-3:]
    total = mine[...]
    for part in parts:
        total += part[...].astype(F32)
    lanes = total.shape[1]
    groups = in_share.shape[1] // lanes
    for q in range(groups):
        in_share[:, q * lanes : (q + 1) * lanes] = total[q * share : (q + 1) * share]
    out_share[...] = total[groups * share : (groups + 1) * share]
    row = jnp.sum(total[(groups + 1) * share :], axis=0, keepdims=True)
    place = lax.axis_index("mem")
    picked = row[:, :share]
    for k in range(1, lanes // share):
        picked = jnp.where(place == k, row[:, k * share : (k + 1) * share], picked)
    bias_share[...] = picked


def finish(mine, parts, share, width):
    lanes = mine.shape[1]
    whole = pl.BlockSpec(memory_space=pltpu.VMEM)
    return pl.pallas_call(
        partial(finish_body, share),
        in_specs=[whole] * (1 + len(parts)),
        out_specs=[whole] * 3,
        out_shape=[
            jax.ShapeDtypeStruct((share, width), F32),
            jax.ShapeDtypeStruct((share, lanes), F32),
            jax.ShapeDtypeStruct((1, share), F32),
        ],
        compiler_params=pltpu.CompilerParams(vmem_limit_bytes=SMALL_LIMIT),
        name="finish",
    )(mine, *parts)


def tie_body(value, after, tied):
    pass


def tie(value, after):
    anywhere = pl.BlockSpec(memory_space=pl.ANY)
    return pl.pallas_call(
        tie_body,
        in_specs=[anywhere] * 2,
        out_specs=anywhere,
        out_shape=jax.ShapeDtypeStruct(value.shape, value.dtype),
        input_output_aliases={0: 0},
        compiler_params=pltpu.CompilerParams(vmem_limit_bytes=TINY_LIMIT),
        name="tie",
    )(value, after)


def area_of(lat_row, rows_total):
    return jnp.cos(jnp.pi * (lat_row.astype(F32) + 0.5) / rows_total - jnp.pi / 2)


def swap_members(block, bit):
    size = lax.axis_size("mem")
    return lax.ppermute(block, "mem", [(i, i ^ bit) for i in range(size)])


def swap_points(block, dz, dx):
    points, members = lax.axis_size("pts"), lax.axis_size("mem")
    pairs = [
        (z * members + m, (z ^ dz) * members + (m ^ (2 * dx)))
        for z in range(points)
        for m in range(members)
    ]
    return lax.ppermute(block, ("pts", "mem"), pairs)


CHUNKS = (288, 288, 256, 192)


def chunks_of(points):
    scale = points // sum(CHUNKS)
    first = 0
    for size in CHUNKS:
        yield first, size * scale
        first += size * scale


def local(latents, member_seeds, targets, lat_row, weight_in, bias_in, weight_out):
    points = latents.shape[1]
    depth = latents.shape[2]
    width, variables = weight_out.shape
    devices_pts, devices_mem = lax.axis_size("pts"), lax.axis_size("mem")
    dests = devices_pts * devices_mem
    loss_coef = LOSS_SCALE / math.sqrt(points * devices_pts)
    area = jnp.broadcast_to(area_of(lat_row, LAT_ROWS)[:, None], (points, variables))
    packed = dests == 16 and devices_mem == 4
    plan = list(chunks_of(points))
    bits = [1 << k for k in reversed(range(devices_mem.bit_length() - 1))]
    saved = []
    out = None
    arrays = [member_seeds, bias_in[None, :], latents, weight_in, weight_out]
    for first, size in plan:
        out, hidden, slope, *staged = forward(arrays, first, size, after=out)
        arrays = staged or arrays
        saved.append([[out, swap_members(out, bits[0])], hidden, slope])
    total = None
    sums = []
    for k, (first, size) in enumerate(plan):
        held, hidden, slope = saved[k]
        if k and LAGS[k - 1] < k:
            held[1] = tie(held[1], sums[k - 1 - LAGS[k - 1]])
        for bit in bits[1:]:
            held = held + [swap_members(v, bit) for v in held]
        last = first + size == points
        total = list(backward(
            held[0], held[1:], targets, area, hidden, slope, arrays[1], arrays[3], total,
            first, loss_coef, dests if last and packed else 0,
            after=saved[-1][0][0] if k == 0 else None,
        ))
        sums.append(total[-1])
    if not packed:
        scatter = lambda v: lax.psum_scatter(v, ("pts", "mem"), scatter_dimension=0, tiled=True)
        return scatter(total[0]), scatter(total[1]), scatter(jnp.sum(total[2], axis=0))
    keep, send = total
    arrived = swap_members(send, 1)
    mine, *parts = spread_out(keep, arrived, LINK)
    parts = [swap_points(part, dz, dx) for part, (dz, dx) in zip(parts, OFFSETS)]
    in_share, out_share, bias_share = finish(mine, parts, depth // dests, width)
    return in_share, out_share, bias_share.reshape(depth // dests)


def solution(mesh):
    return jax.shard_map(
        local,
        mesh=mesh,
        in_specs=(
            P("mem", ("groups", "pts"), None),
            P(("groups", "mem")),
            P(("groups", "pts"), None),
            P(("groups", "pts")),
            P(),
            P(),
            P(),
        ),
        out_specs=(
            P(("groups", "pts", "mem"), None),
            P(("groups", "pts", "mem"), None),
            P(("groups", "pts", "mem")),
        ),
        check_vma=False,
    )
```
